256 devices in a mesh: tm: 16 (over y_hi, z), space: 16 (over x, y_lo, core).
Axes of the slice: x: 4, y: 4 (y_hi: 2, y_lo: 2; y = y_hi * 2 + y_lo), z: 8, core: 2. Of those that a mesh axis runs over, the one named last changes fastest.
Arguments:
- query: bfloat16 [16, 16, 384, 1536], P('tm', 'space'), may hold values from -6 to 6
- fresh_key: bfloat16 [16, 16, 384, 1536], P('tm', 'space'), may hold values from -6 to 6
- fresh_value: bfloat16 [16, 16, 384, 1536], P('tm', 'space'), may hold values from -6 to 6
- stale_kv: bfloat16 [2, 16, 16, 384, 1536], P(None, 'tm', 'space'), may hold values from -6 to 6
- text_kv: bfloat16 [2, 256, 1536], P(None, 'space'), may hold values from -6 to 6
- window: int32 [12, 2], replicated, may hold values from 0 to 1, as said below
- text_len: int32 [1], replicated, may hold values from 64 to 256
Outputs:
- attended: bfloat16 [16, 16, 384, 1536], P('tm', 'space')
The draws below stay inside these ranges and needn't reach their ends.
Inputs may be any that keep to these rules, and one draw needn't show every extreme that they name: `window`: each of the four pairs of reaches (0 or 1 along frames, 0 or 1 along space) belongs to exactly 3 heads.
All inputs are finite; a program needn't handle non-finite values.
Results may differ from the reference program's by a relative error of at most 0.0046.
Values may be sent and summed in bfloat16 or wider, within the bound.
A program may use at most 128 MiB of HBM per device.

```python
import math
import jax
import jax.numpy as jnp
from jax import lax

HEADS = 12
TEXT = 256
TOK_DEV = 384
WIDTH = 1536
TILES_T = 16
TILES_S = 16


def draw_query(key, part):
    key = jax.random.fold_in(key, 11)
    base = jnp.clip(jax.random.normal(key, (TILES_T, TILES_S, TOK_DEV, WIDTH), jnp.float32), -4.0, 4.0)
    return base.astype(jnp.bfloat16)


def draw_fresh_key(key, part):
    key = jax.random.fold_in(key, 23)
    base = jnp.clip(jax.random.normal(key, (TILES_T, TILES_S, TOK_DEV, WIDTH), jnp.float32), -4.0, 4.0)
    return base.astype(jnp.bfloat16)


def draw_window(key, part):
    key = jax.random.fold_in(key, 5)
    order = jax.random.permutation(key, HEADS)
    combo = order % 4
    return jnp.stack([combo // 2, combo % 2], axis=1).astype(jnp.int32)


def steps_of(key, shape, split, least, top_value):
    loudness = 1.0
    for axis_at, shards_of in split:
        heights = jax.random.uniform(jax.random.fold_in(jax.random.fold_in(key, 6), axis_at), (shards_of,), jnp.float32, least / len(split), top_value / len(split))
        loudness = loudness * jnp.repeat(jnp.exp(heights), shape[axis_at] // shards_of).reshape((-1,) + (1,) * (len(shape) - 1 - axis_at))
    return loudness


def bell_draw(rng, dims, scale, bound, pieces=(), kind=jnp.bfloat16):
    values = jax.random.normal(rng, dims, jnp.float32) * scale
    if len(pieces) > 0:
        values = steps_of(rng, dims, pieces, -0.22, 0.18) * values
    return jnp.clip(values, min=-bound, max=bound).astype(kind)


def setup_inputs(seed: int = 0) -> dict:
    arg_keys = jax.random.split(jax.random.key(seed), 8)
    return {
        "query": draw_query(jax.random.fold_in(arg_keys[7], 71), 0),
        "fresh_key": draw_fresh_key(jax.random.fold_in(arg_keys[7], 71), 0),
        "fresh_value": bell_draw(arg_keys[2], (TILES_T, TILES_S, TOK_DEV, WIDTH), 1.0, 6.0, ((0, 16), (1, 16))),
        "stale_kv": bell_draw(arg_keys[3], (2, TILES_T, TILES_S, TOK_DEV, WIDTH), 1.0, 6.0, ((1, 16), (2, 16))),
        "text_kv": bell_draw(arg_keys[4], (2, TEXT, WIDTH), 1.0, 6.0, ((1, 16),)),
        "window": draw_window(jax.random.fold_in(arg_keys[7], 71), 0),
        "text_len": jax.random.randint(arg_keys[6], (1,), TEXT // 4, TEXT + 1).astype(jnp.int32),
    }


def attend_tile(query_rows, key_rows, value_rows, slot_valid, window, text_len):
    tile_rows = query_rows.shape[0]
    width = query_rows.shape[1]
    heads = window.shape[0]
    head_dim = width // heads
    scale = 1.0 / math.sqrt(head_dim)
    near_count = 9 * tile_rows
    text_rows = key_rows.shape[0] - near_count
    tile_of = jnp.arange(near_count, dtype=jnp.int32) // tile_rows
    step_time = tile_of // 3 - 1
    step_space = tile_of % 3 - 1
    tile_valid = slot_valid[tile_of]
    text_valid = jnp.arange(text_rows, dtype=jnp.int32) < text_len[0]
    query_heads = query_rows.reshape(tile_rows, heads, head_dim).transpose(1, 0, 2)
    key_heads = key_rows.reshape(-1, heads, head_dim).transpose(1, 0, 2)
    value_heads = value_rows.reshape(-1, heads, head_dim).transpose(1, 0, 2)

    def one_head(packed):
        query_head, key_head, value_head, reach = packed
        near_ok = tile_valid & (jnp.abs(step_time) <= reach[0]) & (jnp.abs(step_space) <= reach[1])
        allowed = jnp.concatenate([near_ok, text_valid])
        scores = jnp.dot(query_head, key_head.T, preferred_element_type=jnp.float32) * scale
        masked = jnp.where(allowed[None, :], scores, -1e+30)
        peak = lax.optimization_barrier(jnp.max(masked, axis=1, keepdims=True))
        weights = jnp.where(allowed[None, :], jnp.exp(masked - peak), 0.0)
        total = lax.optimization_barrier(jnp.sum(weights, axis=1, keepdims=True))
        mixed = jnp.dot(weights.astype(jnp.bfloat16), value_head, preferred_element_type=jnp.float32)
        return mixed / total
    result = lax.map(one_head, (query_heads, key_heads, value_heads, window))
    return result.transpose(1, 0, 2).reshape(tile_rows, width).astype(jnp.bfloat16)

def tile_output(block, query_rows, key_here, value_here, time_pos, space_pos, time_tiles, space_tiles, text_both, window, text_len):
    tile_rows, width = query_rows.shape
    near_keys = block[0].reshape(9, tile_rows, width).at[4].set(key_here).reshape(9 * tile_rows, width)
    near_values = block[1].reshape(9, tile_rows, width).at[4].set(value_here).reshape(9 * tile_rows, width)
    key_rows = jnp.concatenate([near_keys, text_both[0]], axis=0)
    value_rows = jnp.concatenate([near_values, text_both[1]], axis=0)
    offsets = jnp.arange(3, dtype=jnp.int32) - 1
    time_ok = (time_pos + offsets >= 0) & (time_pos + offsets < time_tiles)
    space_ok = (space_pos + offsets >= 0) & (space_pos + offsets < space_tiles)
    slot_valid = (time_ok[:, None] & space_ok[None, :]).reshape(9)
    return attend_tile(query_rows, key_rows, value_rows, slot_valid, window, text_len)

def reference(query, fresh_key, fresh_value, stale_kv, text_kv, window, text_len):
    padded = jnp.pad(stale_kv, ((0, 0), (1, 1), (1, 1), (0, 0), (0, 0)))
    anchor = jnp.int32(0)

    def one_tile(index):
        time_pos = (index // TILES_S).astype(jnp.int32)
        space_pos = (index % TILES_S).astype(jnp.int32)
        block = lax.dynamic_slice(padded, (anchor, time_pos, space_pos, anchor, anchor), (2, 3, 3, TOK_DEV, WIDTH))
        start = (time_pos, space_pos, anchor, anchor)
        query_rows = lax.dynamic_slice(query, start, (1, 1, TOK_DEV, WIDTH))[0, 0]
        key_here = lax.dynamic_slice(fresh_key, start, (1, 1, TOK_DEV, WIDTH))[0, 0]
        value_here = lax.dynamic_slice(fresh_value, start, (1, 1, TOK_DEV, WIDTH))[0, 0]
        return tile_output(block, query_rows, key_here, value_here, time_pos, space_pos, TILES_T, TILES_S, text_kv, window, text_len)
    tiles = lax.map(one_tile, jnp.arange(TILES_T * TILES_S, dtype=jnp.int32))
    return tiles.reshape(TILES_T, TILES_S, TOK_DEV, WIDTH)
```

```python
import math

import jax
import jax.numpy as jnp
from jax import lax
from jax.experimental import pallas as pl
from jax.experimental.pallas import tpu as pltpu
from jax.sharding import PartitionSpec as P

MESH = pl.DeviceIdType.MESH
HEAD = 128
GROUP = 3
HEADS = 12
LANES = 128
ROW_BLOCK = 384


def kernel(
    query, fresh_key, fresh_value, stale, text, window, text_len, out,
    q_all, k_all, v_all, stale_all, words, out_all,
    pack11, pack10, pack01, packq,
    got11, got10, got01, gotq,
    o_send, o_stat, o_got, o_got_stat,
    peak, total, mixed, done, order, place,
    load_sem, send_sem, recv_sem, text_send, text_recv,
):
    rows = q_all.shape[1]
    times = lax.axis_size("tm")
    spaces = lax.axis_size("space")
    time = lax.axis_index("tm")
    space = lax.axis_index("space")
    core = lax.rem(space, 2)
    low = lax.rem(space // 2, 2)
    column = space // 4
    has_time = (time > 0, time < times - 1)
    has_space = (space > 0, space < spaces - 1)
    next_time = (time - 1, time + 1)
    next_space = (space - 1, space + 1)
    scale = math.log2(math.e) / math.sqrt(HEAD)

    mine = words.at[core, column, low]
    for head in range(HEADS):
        at = pl.ds(head * HEAD, HEAD)
        pltpu.make_async_copy(stale.at[:, :, at], stale_all.at[head], load_sem.at[0]).start()
    for head in range(HEADS):
        at = pl.ds(head * HEAD, HEAD)
        pltpu.make_async_copy(query.at[:, at], q_all.at[head], load_sem.at[1]).start()
        pltpu.make_async_copy(text.at[:, :, at], mine.at[head], load_sem.at[2]).start()
    for head in range(HEADS):
        at = pl.ds(head * HEAD, HEAD)
        pltpu.make_async_copy(fresh_key.at[:, at], k_all.at[head], load_sem.at[3]).start()
        pltpu.make_async_copy(fresh_value.at[:, at], v_all.at[head], load_sem.at[4]).start()
    loads = [
        pltpu.make_async_copy(target, target, load_sem.at[i])
        for i, target in enumerate((stale_all, q_all, mine, k_all, v_all))
    ]

    partner_low = column * 4 + (1 - low) * 2 + core
    sibling = space + 1 - 2 * core
    barrier = pltpu.get_barrier_semaphore()
    partners = [
        {"tm": lax.rem(time + 1, times)},
        {"tm": lax.rem(time + times - 1, times)},
        {"space": lax.rem(space + 1, spaces)},
        {"space": lax.rem(space + spaces - 1, spaces)},
        {"space": partner_low},
    ] + [{"space": lax.rem(space + 4 * d, spaces)} for d in (1, 2, 3)]
    for partner in partners:
        pl.semaphore_signal(barrier, inc=1, device_id=partner, device_id_type=MESH)

    counts = [jnp.int32(0)] * 4
    slots = []
    for head in range(HEADS):
        reach_time, reach_space = window[head, 0], window[head, 1]
        both = reach_time * reach_space
        hits = [both, reach_time - both, reach_space - both, 1 - reach_time - reach_space + both]
        slot = jnp.int32(0)
        for k in range(4):
            slot = slot + hits[k] * (GROUP * k + counts[k])
            counts[k] = counts[k] + hits[k]
        slots.append(slot)
        place[head] = jnp.minimum(slot, HEADS - 1)
    for s in range(HEADS):
        chosen = jnp.int32(0)
        for head in range(HEADS):
            apart = jnp.maximum(slots[head] - s, s - slots[head])
            chosen = chosen + head * jnp.maximum(1 - apart, 0)
        order[s] = chosen

    def pack(target, base):
        for g in range(GROUP):
            target[:, g] = stale_all[order[base + g]]

    def along_time(kind, d, source, target):
        return pltpu.make_async_remote_copy(
            src_ref=source, dst_ref=target.at[1 - d],
            send_sem=send_sem.at[kind, d], recv_sem=recv_sem.at[kind, 1 - d],
            device_id={"tm": time - 1 + 2 * d}, device_id_type=MESH,
        )

    def along_space(kind, d, source, target):
        return pltpu.make_async_remote_copy(
            src_ref=source, dst_ref=target.at[1 - d],
            send_sem=send_sem.at[kind, d], recv_sem=recv_sem.at[kind, 1 - d],
            device_id={"space": space - 1 + 2 * d}, device_id_type=MESH,
        )

    def send_both(has, make, kind, source, target):
        for d in (0, 1):
            @pl.when(has[d])
            def _():
                make(kind, d, source, target).start()

    def arrived(has, make, kind, source, target):
        for d in (0, 1):
            @pl.when(has[d])
            def _():
                make(kind, 1 - d, source, target).wait_recv()

    def sent(has, make, kind, source, target):
        for d in (0, 1):
            @pl.when(has[d])
            def _():
                make(kind, d, source, target).wait_send()

    loads[0].wait()
    pack(pack11, 0)
    pl.semaphore_wait(barrier, len(partners))
    send_both(has_time, along_time, 0, pack11, got11)
    loads[1].wait()
    for g in range(GROUP):
        packq[g] = q_all[order[g]]
    send_both(has_space, along_space, 3, packq, gotq)
    loads[2].wait()
    swap = pltpu.make_async_remote_copy(
        src_ref=mine, dst_ref=mine, send_sem=text_send.at[0], recv_sem=text_recv.at[0],
        device_id={"space": partner_low}, device_id_type=MESH,
    )
    swap.start()
    pack(pack01, 2 * GROUP)
    send_both(has_space, along_space, 2, pack01, got01)
    pack(pack10, GROUP)
    send_both(has_time, along_time, 1, pack10, got10)

    swap.wait_recv()
    pair = words.at[core, column]
    spread = [
        pltpu.make_async_remote_copy(
            src_ref=pair, dst_ref=pair, send_sem=text_send.at[d], recv_sem=text_recv.at[d],
            device_id={"space": lax.rem(space + 4 * d, spaces)}, device_id_type=MESH,
        )
        for d in (1, 2, 3)
    ]
    for copy in spread:
        copy.start()

    def attend(state, query_rows, keys, values, first=False, live=None):
        ones = jnp.ones((keys.shape[0], LANES), jnp.bfloat16)
        values = jnp.concatenate([values, ones], axis=1)
        parts = keys.shape[0] // LANES
        for at in range(0, rows, ROW_BLOCK):
            here = pl.ds(at, ROW_BLOCK)
            scores = lax.dot_general(
                query_rows[at : at + ROW_BLOCK], keys, (((1,), (1,)), ((), ())),
                preferred_element_type=jnp.float32,
            ) * scale
            if live is not None:
                scores = jnp.where(live, scores, -1e30)
            top = jnp.broadcast_to(jnp.max(scores, axis=1, keepdims=True), (ROW_BLOCK, LANES))
            if not first:
                before = peak[state, here]
                top = jnp.maximum(before, top)
            weights = jnp.exp2(scores - jnp.concatenate([top] * parts, axis=1)).astype(jnp.bfloat16)
            both = jnp.dot(weights, values, preferred_element_type=jnp.float32)
            peak[state, here] = top
            if first:
                mixed[state, here] = both[:, :HEAD]
                total[state, here] = both[:, HEAD:]
            else:
                shrink = jnp.exp2(before - top)
                mixed[state, here] = mixed[state, here] * shrink + both[:, :HEAD]
                total[state, here] = total[state, here] * shrink + both[:, HEAD:]

    def own_query(slot):
        return q_all[order[slot]]

    loads[3].wait()
    loads[4].wait()

    @pl.loop(0, HEADS)
    def _(slot):
        head = order[slot]
        attend(slot, q_all[head], k_all[head], v_all[head], first=True)

    arrived(has_space, along_space, 3, packq, gotq)

    def side_ok(d, position, count):
        return jnp.where(d == 0, position > 0, position < count - 1)

    @pl.loop(0, 2)
    def _(d):
        @pl.when(side_ok(d, space, spaces))
        def _():
            @pl.loop(0, GROUP)
            def _(g):
                attend(HEADS + d * GROUP + g, gotq[d, g], pack11[0, g], pack11[1, g], first=True)

    for copy in spread:
        copy.wait_recv()
    half = words.at[core]
    across = pltpu.make_async_remote_copy(
        src_ref=half, dst_ref=half, send_sem=text_send.at[4], recv_sem=text_recv.at[4],
        device_id={"space": sibling}, device_id_type=MESH,
    )
    across.start()
    across.wait_recv()
    count = 2 * spaces // 2 * words.shape[5]
    index = lax.broadcasted_iota(jnp.int32, (1, count), 1)
    token = (((index // 32) % 4) * 4 + ((index // 16) % 2) * 2 + index // 128) * 16 + index % 16
    live = token < text_len[0]

    @pl.loop(0, HEADS)
    def _(slot):
        head = order[slot]
        keys = words[:, :, :, head, 0].reshape(count, HEAD)
        values = words[:, :, :, head, 1].reshape(count, HEAD)
        attend(slot, q_all[head], keys, values, live=live)

    arrived(has_time, along_time, 0, pack11, got11)
    lane = lax.broadcasted_iota(jnp.int32, (rows, LANES), 1)

    @pl.loop(0, 2)
    def _(i):
        d = lax.rem(i + core, 2)

        @pl.when(side_ok(d, space, spaces))
        def _():
            @pl.loop(0, GROUP)
            def _(g):
                state = HEADS + d * GROUP + g

                @pl.loop(0, 2)
                def _(e):
                    @pl.when(side_ok(e, time, times))
                    def _():
                        attend(state, gotq[d, g], got11[e, 0, g], got11[e, 1, g])

                o_send[d, g] = (mixed[state] / total[state]).astype(jnp.bfloat16)

            stats = jnp.zeros((rows, LANES), jnp.float32)
            for g in range(GROUP):
                state = HEADS + d * GROUP + g
                stats = jnp.where(lane == g, peak[state] + jnp.log2(total[state]), stats)
            o_stat[d] = stats.T[:8]
            along_space(4, d, o_send.at[d], o_got).start()
            along_space(5, d, o_stat.at[d], o_got_stat).start()

    @pl.loop(0, 2)
    def _(e):
        @pl.when(side_ok(e, time, times))
        def _():
            @pl.loop(0, GROUP)
            def _(g):
                attend(g, own_query(g), got11[e, 0, g], got11[e, 1, g])

    arrived(has_space, along_space, 2, pack01, got01)

    @pl.loop(0, 2)
    def _(e):
        @pl.when(side_ok(e, space, spaces))
        def _():
            @pl.loop(0, GROUP)
            def _(g):
                attend(2 * GROUP + g, own_query(2 * GROUP + g), got01[e, 0, g], got01[e, 1, g])

    arrived(has_time, along_time, 1, pack10, got10)

    @pl.loop(0, 2)
    def _(e):
        @pl.when(side_ok(e, time, times))
        def _():
            @pl.loop(0, GROUP)
            def _(g):
                attend(GROUP + g, own_query(GROUP + g), got10[e, 0, g], got10[e, 1, g])

    @pl.loop(GROUP, HEADS)
    def _(slot):
        done[slot] = (mixed[slot] / total[slot]).astype(jnp.bfloat16)

    for d in (0, 1):
        @pl.when(has_space[d])
        def _():
            along_space(4, 1 - d, o_send.at[1 - d], o_got).wait_recv()
            along_space(5, 1 - d, o_stat.at[1 - d], o_got_stat).wait_recv()
            spare = jnp.zeros((LANES - 8, rows), jnp.float32)
            stats = jnp.concatenate([o_got_stat[d], spare], axis=0).T
            for g in range(GROUP):
                other = jnp.broadcast_to(stats[:, g : g + 1], (rows, LANES))
                before = peak[g]
                top = jnp.maximum(before, other)
                keep = jnp.exp2(before - top)
                add = jnp.exp2(other - top)
                peak[g] = top
                mixed[g] = mixed[g] * keep + o_got[d, g].astype(jnp.float32) * add
                total[g] = total[g] * keep + add

    for g in range(GROUP):
        done[g] = (mixed[g] / total[g]).astype(jnp.bfloat16)
    for head in range(HEADS):
        out_all[:, head * HEAD : (head + 1) * HEAD] = done[place[head]]
    store = pltpu.make_async_copy(out_all, out, load_sem.at[5])
    store.start()

    sent(has_time, along_time, 0, pack11, got11)
    sent(has_time, along_time, 1, pack10, got10)
    sent(has_space, along_space, 2, pack01, got01)
    sent(has_space, along_space, 3, packq, gotq)
    for d in (0, 1):
        @pl.when(has_space[d])
        def _():
            along_space(4, d, o_send.at[d], o_got).wait_send()
            along_space(5, d, o_stat.at[d], o_got_stat).wait_send()
    swap.wait_send()
    for copy in spread:
        copy.wait_send()
    across.wait_send()
    store.wait()


def on_device(query, fresh_key, fresh_value, stale_kv, text_kv, window, text_len):
    rows, width = query.shape[2:]
    words = text_kv.shape[1]
    bf16, f32 = jnp.bfloat16, jnp.float32
    heads = (GROUP, rows, HEAD)
    anywhere = pl.BlockSpec(memory_space=pl.ANY)
    scalars = pl.BlockSpec(memory_space=pltpu.SMEM)
    result = pl.pallas_call(
        kernel,
        out_shape=jax.ShapeDtypeStruct((rows, width), bf16),
        in_specs=[anywhere] * 5 + [scalars] * 2,
        out_specs=anywhere,
        scratch_shapes=[
            pltpu.VMEM((HEADS, rows, HEAD), bf16),
            pltpu.VMEM((HEADS, rows, HEAD), bf16),
            pltpu.VMEM((HEADS, rows, HEAD), bf16),
            pltpu.VMEM((HEADS, 2, rows, HEAD), bf16),
            pltpu.VMEM((2, 4, 2, HEADS, 2, words, HEAD), bf16),
            pltpu.VMEM((rows, width), bf16),
            pltpu.VMEM((2, *heads), bf16),
            pltpu.VMEM((2, *heads), bf16),
            pltpu.VMEM((2, *heads), bf16),
            pltpu.VMEM(heads, bf16),
            pltpu.VMEM((2, 2, *heads), bf16),
            pltpu.VMEM((2, 2, *heads), bf16),
            pltpu.VMEM((2, 2, *heads), bf16),
            pltpu.VMEM((2, *heads), bf16),
            pltpu.VMEM((2, *heads), bf16),
            pltpu.VMEM((2, 8, rows), f32),
            pltpu.VMEM((2, *heads), bf16),
            pltpu.VMEM((2, 8, rows), f32),
            pltpu.VMEM((HEADS + 2 * GROUP, rows, LANES), f32),
            pltpu.VMEM((HEADS + 2 * GROUP, rows, LANES), f32),
            pltpu.VMEM((HEADS + 2 * GROUP, rows, HEAD), f32),
            pltpu.VMEM((HEADS, rows, HEAD), bf16),
            pltpu.SMEM((HEADS,), jnp.int32),
            pltpu.SMEM((HEADS,), jnp.int32),
            pltpu.SemaphoreType.DMA((6,)),
            pltpu.SemaphoreType.DMA((6, 2)),
            pltpu.SemaphoreType.DMA((6, 2)),
            pltpu.SemaphoreType.DMA((5,)),
            pltpu.SemaphoreType.DMA((5,)),
        ],
        compiler_params=pltpu.CompilerParams(
            collective_id=0, has_side_effects=True, vmem_limit_bytes=50 << 20
        ),
    )(
        query[0, 0], fresh_key[0, 0], fresh_value[0, 0], stale_kv[:, 0, 0], text_kv,
        window, text_len,
    )
    return result[None, None]


def solution(mesh):
    in_specs = (
        P("tm", "space", None, None),
        P("tm", "space", None, None),
        P("tm", "space", None, None),
        P(None, "tm", "space", None, None),
        P(None, "space", None),
        P(),
        P(),
    )
    out_specs = P("tm", "space", None, None)
    return jax.shard_map(
        on_device, mesh=mesh, in_specs=in_specs, out_specs=out_specs, check_vma=False
    )
```

```python
import functools
import math

import jax
import jax.numpy as jnp
from jax import lax
from jax.experimental import pallas as pl
from jax.experimental.pallas import tpu as pltpu
from jax.sharding import PartitionSpec as P

MESH = pl.DeviceIdType.MESH
HEAD = 128
GROUP = 3
HEADS = 12
LANES = 128
ROW_BLOCK = 384


def kernel(
    query, fresh_key, fresh_value, stale, text, window, text_len, out,
    q_all, k_all, v_all, stale_all, words, out_all,
    pack11, pack10, pack01, packq,
    got11, got10, got01, gotq,
    o_send, o_stat, o_got, o_got_stat,
    peak, total, mixed, done, order, place,
    load_sem, send_sem, recv_sem, text_send, text_recv,
):
    rows = q_all.shape[1]
    times = lax.axis_size("tm")
    spaces = lax.axis_size("space")
    time = lax.axis_index("tm")
    space = lax.axis_index("space")
    core = lax.rem(space, 2)
    low = lax.rem(space // 2, 2)
    column = space // 4
    has_time = (time > 0, time < times - 1)
    has_space = (space > 0, space < spaces - 1)
    next_time = (time - 1, time + 1)
    next_space = (space - 1, space + 1)
    scale = math.log2(math.e) / math.sqrt(HEAD)

    mine = words.at[core, column, low]
    for head in range(HEADS):
        at = pl.ds(head * HEAD, HEAD)
        pltpu.make_async_copy(stale.at[:, :, at], stale_all.at[head], load_sem.at[0]).start()
    for head in range(HEADS):
        at = pl.ds(head * HEAD, HEAD)
        pltpu.make_async_copy(query.at[:, at], q_all.at[head], load_sem.at[1]).start()
        pltpu.make_async_copy(text.at[:, :, at], mine.at[head], load_sem.at[2]).start()
    for head in range(HEADS):
        at = pl.ds(head * HEAD, HEAD)
        pltpu.make_async_copy(fresh_key.at[:, at], k_all.at[head], load_sem.at[3]).start()
        pltpu.make_async_copy(fresh_value.at[:, at], v_all.at[head], load_sem.at[4]).start()
    loads = [
        pltpu.make_async_copy(target, target, load_sem.at[i])
        for i, target in enumerate((stale_all, q_all, mine, k_all, v_all))
    ]

    partner_low = column * 4 + (1 - low) * 2 + core
    sibling = space + 1 - 2 * core
    barrier = pltpu.get_barrier_semaphore()
    partners = [
        {"tm": lax.rem(time + 1, times)},
        {"tm": lax.rem(time + times - 1, times)},
        {"space": lax.rem(space + 1, spaces)},
        {"space": lax.rem(space + spaces - 1, spaces)},
        {"space": partner_low},
    ] + [{"space": lax.rem(space + 4 * d, spaces)} for d in (1, 2, 3)]
    for partner in partners:
        pl.semaphore_signal(barrier, inc=1, device_id=partner, device_id_type=MESH)

    counts = [jnp.int32(0)] * 4
    slots = []
    for head in range(HEADS):
        reach_time, reach_space = window[head, 0], window[head, 1]
        both = reach_time * reach_space
        hits = [both, reach_time - both, reach_space - both, 1 - reach_time - reach_space + both]
        slot = jnp.int32(0)
        for k in range(4):
            slot = slot + hits[k] * (GROUP * k + counts[k])
            counts[k] = counts[k] + hits[k]
        slots.append(slot)
        place[head] = jnp.minimum(slot, HEADS - 1)
    for s in range(HEADS):
        chosen = jnp.int32(0)
        for head in range(HEADS):
            apart = jnp.maximum(slots[head] - s, s - slots[head])
            chosen = chosen + head * jnp.maximum(1 - apart, 0)
        order[s] = chosen

    def pack(target, base):
        for g in range(GROUP):
            target[:, g] = stale_all[order[base + g]]

    def along_time(kind, d, source, target):
        return pltpu.make_async_remote_copy(
            src_ref=source, dst_ref=target.at[1 - d],
            send_sem=send_sem.at[kind, d], recv_sem=recv_sem.at[kind, 1 - d],
            device_id={"tm": time - 1 + 2 * d}, device_id_type=MESH,
        )

    def along_space(kind, d, source, target):
        return pltpu.make_async_remote_copy(
            src_ref=source, dst_ref=target.at[1 - d],
            send_sem=send_sem.at[kind, d], recv_sem=recv_sem.at[kind, 1 - d],
            device_id={"space": space - 1 + 2 * d}, device_id_type=MESH,
        )

    def send_both(has, make, kind, source, target):
        for d in (0, 1):
            @pl.when(has[d])
            def _():
                make(kind, d, source, target).start()

    def arrived(has, make, kind, source, target):
        for d in (0, 1):
            @pl.when(has[d])
            def _():
                make(kind, 1 - d, source, target).wait_recv()

    def sent(has, make, kind, source, target):
        for d in (0, 1):
            @pl.when(has[d])
            def _():
                make(kind, d, source, target).wait_send()

    loads[0].wait()
    pack(pack11, 0)
    pl.semaphore_wait(barrier, len(partners))
    send_both(has_time, along_time, 0, pack11, got11)
    loads[1].wait()
    for g in range(GROUP):
        packq[g] = q_all[order[g]]
    send_both(has_space, along_space, 3, packq, gotq)
    loads[2].wait()
    swap = pltpu.make_async_remote_copy(
        src_ref=mine, dst_ref=mine, send_sem=text_send.at[0], recv_sem=text_recv.at[0],
        device_id={"space": partner_low}, device_id_type=MESH,
    )
    swap.start()
    pack(pack01, 2 * GROUP)
    send_both(has_space, along_space, 2, pack01, got01)
    pack(pack10, GROUP)
    send_both(has_time, along_time, 1, pack10, got10)

    swap.wait_recv()
    pair = words.at[core, column]
    spread = [
        pltpu.make_async_remote_copy(
            src_ref=pair, dst_ref=pair, send_sem=text_send.at[d], recv_sem=text_recv.at[d],
            device_id={"space": lax.rem(space + 4 * d, spaces)}, device_id_type=MESH,
        )
        for d in (1, 2, 3)
    ]
    for copy in spread:
        copy.start()

    def rows_at(block):
        return pl.ds(block * ROW_BLOCK, ROW_BLOCK)

    def attend(jobs):
        for job in jobs:
            job["keys"] = jnp.concatenate([chunk[0] for chunk in job["chunks"]], axis=0)
            values = jnp.concatenate([chunk[1] for chunk in job["chunks"]], axis=0)
            ones = jnp.ones((values.shape[0], LANES), jnp.bfloat16)
            job["values"] = jnp.concatenate([values, ones], axis=1)
        tasks = [dict(job, here=rows_at(block)) for job in jobs for block in range(rows // ROW_BLOCK)]

        def score(task):
            query_rows = task["query"](task["here"])
            task["scores"] = lax.dot_general(
                query_rows, task["keys"], (((1,), (1,)), ((), ())),
                preferred_element_type=jnp.float32,
            ) * scale

        def weigh(task):
            pieces, tops, at = [], [], 0
            before = task["before"](task["here"]) if task["before"] else None
            for keys, _, live, valid in task["chunks"]:
                piece = task["scores"][:, at : at + keys.shape[0]]
                at += keys.shape[0]
                if live is not None:
                    piece = jnp.where(live, piece, -1e30)
                top = jnp.broadcast_to(jnp.max(piece, axis=1, keepdims=True), (ROW_BLOCK, LANES))
                if valid is not None:
                    top = jnp.where(valid, top, -1e30)
                pieces.append(piece)
                tops.append(top)
            top = functools.reduce(jnp.maximum, tops + ([before[0]] if before else []))
            weights = []
            for piece, (_, _, _, valid) in zip(pieces, task["chunks"]):
                base = top if valid is None else jnp.where(valid, top, 1e30)
                base = jnp.concatenate([base] * (piece.shape[1] // LANES), axis=1)
                weights.append(jnp.exp2(piece - base).astype(jnp.bfloat16))
            both = jnp.dot(
                jnp.concatenate(weights, axis=1), task["values"], preferred_element_type=jnp.float32
            )
            mixed, total = both[:, :HEAD], both[:, HEAD:]
            if before:
                shrink = jnp.exp2(before[0] - top)
                total = before[1] * shrink + total
                mixed = before[2] * shrink + mixed
            task["after"](task["here"], top, total, mixed)

        score(tasks[0])
        for i, task in enumerate(tasks):
            if i + 1 < len(tasks):
                score(tasks[i + 1])
            weigh(task)

    def job(query, chunks, after, before=None):
        return {"query": query, "chunks": chunks, "before": before, "after": after}

    def own(slot):
        head = order[slot]
        return lambda here: q_all[head, here]

    def saved(g, state):
        return lambda here: (peak[g][state, here], total[g][state, here], mixed[g][state, here])

    def save(g, state):
        def after(here, top, weight, value):
            peak[g][state, here] = top
            total[g][state, here] = weight
            mixed[g][state, here] = value

        return after

    def finish(target, at):
        def after(here, top, weight, value):
            target[(*at, here)] = (value / weight).astype(jnp.bfloat16)

        return after

    def fresh(slot):
        head = order[slot]
        return k_all[head], v_all[head], None, None

    def spoken(slot):
        head = order[slot]
        keys = words[:, :, :, head, 0].reshape(count, HEAD)
        values = words[:, :, :, head, 1].reshape(count, HEAD)
        return keys, values, live, None

    def near(got, g, has):
        return [(got[e, 0, g], got[e, 1, g], None, has[e]) for e in (0, 1)]

    def side_ok(d, position, count):
        return jnp.where(d == 0, position > 0, position < count - 1)

    count = 2 * spaces // 2 * words.shape[5]
    index = lax.broadcasted_iota(jnp.int32, (1, count), 1)
    token = (((index // 32) % 4) * 4 + ((index // 16) % 2) * 2 + index // 128) * 16 + index % 16
    live = token < text_len[0]

    for d in (0, 1):
        @pl.when(jnp.logical_not(has_time[d]))
        def _():
            got11[d] = jnp.zeros_like(got11[d])
            got10[d] = jnp.zeros_like(got10[d])

        @pl.when(jnp.logical_not(has_space[d]))
        def _():
            got01[d] = jnp.zeros_like(got01[d])

    loads[3].wait()
    loads[4].wait()

    @pl.loop(0, 3)
    def _(kind):
        attend([
            job(own(kind * GROUP + g), [fresh(kind * GROUP + g)], save(g, kind))
            for g in range(GROUP)
        ])

    arrived(has_space, along_space, 3, packq, gotq)

    def visitor(d, g):
        return lambda here: gotq[d, g, here]

    @pl.loop(0, 2)
    def _(d):
        @pl.when(side_ok(d, space, spaces))
        def _():
            attend([
                job(visitor(d, g), [(pack11[0, g], pack11[1, g], None, None)], save(g, 3 + d))
                for g in range(GROUP)
            ])

    for copy in spread:
        copy.wait_recv()
    half = words.at[core]
    across = pltpu.make_async_remote_copy(
        src_ref=half, dst_ref=half, send_sem=text_send.at[4], recv_sem=text_recv.at[4],
        device_id={"space": sibling}, device_id_type=MESH,
    )
    across.start()
    across.wait_recv()
    attend([
        job(own(3 * GROUP + g), [fresh(3 * GROUP + g), spoken(3 * GROUP + g)], finish(done, (3 * GROUP + g,)))
        for g in range(GROUP)
    ])

    arrived(has_time, along_time, 0, pack11, got11)
    lane = lax.broadcasted_iota(jnp.int32, (rows, LANES), 1)

    @pl.loop(0, 2)
    def _(i):
        d = lax.rem(i + core, 2)

        @pl.when(side_ok(d, space, spaces))
        def _():
            def give(g):
                def after(here, top, weight, value):
                    o_send[d, g, here] = (value / weight).astype(jnp.bfloat16)
                    peak[g][3 + d, here] = top + jnp.log2(weight)

                return after

            attend([
                job(visitor(d, g), near(got11, g, has_time), give(g), saved(g, 3 + d))
                for g in range(GROUP)
            ])
            stats = jnp.zeros((rows, LANES), jnp.float32)
            for g in range(GROUP):
                stats = jnp.where(lane == g, peak[g][3 + d], stats)
            o_stat[d] = stats.T[:8]
            along_space(4, d, o_send.at[d], o_got).start()
            along_space(5, d, o_stat.at[d], o_got_stat).start()

    attend([
        job(own(g), [spoken(g), *near(got11, g, has_time)], save(g, 0), saved(g, 0))
        for g in range(GROUP)
    ])
    arrived(has_space, along_space, 2, pack01, got01)
    attend([
        job(own(2 * GROUP + g), [spoken(2 * GROUP + g), *near(got01, g, has_space)], finish(done, (2 * GROUP + g,)), saved(g, 2))
        for g in range(GROUP)
    ])
    arrived(has_time, along_time, 1, pack10, got10)
    attend([
        job(own(GROUP + g), [spoken(GROUP + g), *near(got10, g, has_time)], finish(done, (GROUP + g,)), saved(g, 1))
        for g in range(GROUP)
    ])

    for d in (0, 1):
        @pl.when(has_space[d])
        def _():
            along_space(4, 1 - d, o_send.at[1 - d], o_got).wait_recv()
            along_space(5, 1 - d, o_stat.at[1 - d], o_got_stat).wait_recv()
            spare = jnp.zeros((LANES - 8, rows), jnp.float32)
            stats = jnp.concatenate([o_got_stat[d], spare], axis=0).T
            for g in range(GROUP):
                other = jnp.broadcast_to(stats[:, g : g + 1], (rows, LANES))
                before = peak[g][0]
                top = jnp.maximum(before, other)
                keep = jnp.exp2(before - top)
                add = jnp.exp2(other - top)
                peak[g][0] = top
                mixed[g][0] = mixed[g][0] * keep + o_got[d, g].astype(jnp.float32) * add
                total[g][0] = total[g][0] * keep + add

    for g in range(GROUP):
        done[g] = (mixed[g][0] / total[g][0]).astype(jnp.bfloat16)
    for head in range(HEADS):
        out_all[:, head * HEAD : (head + 1) * HEAD] = done[place[head]]
    store = pltpu.make_async_copy(out_all, out, load_sem.at[5])
    store.start()

    sent(has_time, along_time, 0, pack11, got11)
    sent(has_time, along_time, 1, pack10, got10)
    sent(has_space, along_space, 2, pack01, got01)
    sent(has_space, along_space, 3, packq, gotq)
    for d in (0, 1):
        @pl.when(has_space[d])
        def _():
            along_space(4, d, o_send.at[d], o_got).wait_send()
            along_space(5, d, o_stat.at[d], o_got_stat).wait_send()
    swap.wait_send()
    for copy in spread:
        copy.wait_send()
    across.wait_send()
    store.wait()


def on_device(query, fresh_key, fresh_value, stale_kv, text_kv, window, text_len):
    rows, width = query.shape[2:]
    words = text_kv.shape[1]
    bf16, f32 = jnp.bfloat16, jnp.float32
    heads = (GROUP, rows, HEAD)
    anywhere = pl.BlockSpec(memory_space=pl.ANY)
    scalars = pl.BlockSpec(memory_space=pltpu.SMEM)
    result = pl.pallas_call(
        kernel,
        out_shape=jax.ShapeDtypeStruct((rows, width), bf16),
        in_specs=[anywhere] * 5 + [scalars] * 2,
        out_specs=anywhere,
        scratch_shapes=[
            pltpu.VMEM((HEADS, rows, HEAD), bf16),
            pltpu.VMEM((HEADS, rows, HEAD), bf16),
            pltpu.VMEM((HEADS, rows, HEAD), bf16),
            pltpu.VMEM((HEADS, 2, rows, HEAD), bf16),
            pltpu.VMEM((2, 4, 2, HEADS, 2, words, HEAD), bf16),
            pltpu.VMEM((rows, width), bf16),
            pltpu.VMEM((2, *heads), bf16),
            pltpu.VMEM((2, *heads), bf16),
            pltpu.VMEM((2, *heads), bf16),
            pltpu.VMEM(heads, bf16),
            pltpu.VMEM((2, 2, *heads), bf16),
            pltpu.VMEM((2, 2, *heads), bf16),
            pltpu.VMEM((2, 2, *heads), bf16),
            pltpu.VMEM((2, *heads), bf16),
            pltpu.VMEM((2, *heads), bf16),
            pltpu.VMEM((2, 8, rows), f32),
            pltpu.VMEM((2, *heads), bf16),
            pltpu.VMEM((2, 8, rows), f32),
            [pltpu.VMEM((5, rows, LANES), f32)] * GROUP,
            [pltpu.VMEM((5, rows, LANES), f32)] * GROUP,
            [pltpu.VMEM((5, rows, HEAD), f32)] * GROUP,
            pltpu.VMEM((HEADS, rows, HEAD), bf16),
            pltpu.SMEM((HEADS,), jnp.int32),
            pltpu.SMEM((HEADS,), jnp.int32),
            pltpu.SemaphoreType.DMA((6,)),
            pltpu.SemaphoreType.DMA((6, 2)),
            pltpu.SemaphoreType.DMA((6, 2)),
            pltpu.SemaphoreType.DMA((5,)),
            pltpu.SemaphoreType.DMA((5,)),
        ],
        compiler_params=pltpu.CompilerParams(
            collective_id=0, has_side_effects=True, vmem_limit_bytes=60 << 20
        ),
    )(
        query[0, 0], fresh_key[0, 0], fresh_value[0, 0], stale_kv[:, 0, 0], text_kv,
        window, text_len,
    )
    return result[None, None]


def solution(mesh):
    in_specs = (
        P("tm", "space", None, None),
        P("tm", "space", None, None),
        P("tm", "space", None, None),
        P(None, "tm", "space", None, None),
        P(None, "space", None),
        P(),
        P(),
    )
    out_specs = P("tm", "space", None, None)
    return jax.shard_map(
        on_device, mesh=mesh, in_specs=in_specs, out_specs=out_specs, check_vma=False
    )
```

```python
import functools
import math

import jax
import jax.numpy as jnp
from jax import lax
from jax.experimental import pallas as pl
from jax.experimental.pallas import tpu as pltpu
from jax.sharding import PartitionSpec as P

MESH = pl.DeviceIdType.MESH
HEAD = 128
GROUP = 3
HEADS = 12
LANES = 128
ROW_BLOCK = 384


def kernel(
    query, fresh_key, fresh_value, stale, text, window, text_len, out,
    q_all, k_all, v_all, stale_all, words, out_all,
    pack11, pack10, pack01, packq,
    got11, got10, got01, gotq,
    o_send, o_stat, o_got, o_got_stat,
    peak, total, mixed, done, order, place,
    relay, load_sem, send_sem, recv_sem, text_send, text_recv, relay_send, relay_recv,
):
    rows = q_all.shape[1]
    times = lax.axis_size("tm")
    spaces = lax.axis_size("space")
    time = lax.axis_index("tm")
    space = lax.axis_index("space")
    core = lax.rem(space, 2)
    low = lax.rem(space // 2, 2)
    column = space // 4
    has_time = (time > 0, time < times - 1)
    has_space = (space > 0, space < spaces - 1)
    next_time = (time - 1, time + 1)
    next_space = (space - 1, space + 1)
    middle = times // 2
    first, last = time == 0, time == times - 1
    outer = jnp.logical_or(first, last)
    inner = jnp.logical_or(time == middle - 1, time == middle)
    straight = (
        jnp.logical_and(has_time[0], time != middle),
        jnp.logical_and(has_time[1], time != middle - 1),
    )
    bent = (time == middle, time == middle - 1)
    scale = math.log2(math.e) / math.sqrt(HEAD)

    mine = words.at[core, column, low]
    for head in range(HEADS):
        at = pl.ds(head * HEAD, HEAD)
        pltpu.make_async_copy(stale.at[:, :, at], stale_all.at[head], load_sem.at[0]).start()
    for head in range(HEADS):
        at = pl.ds(head * HEAD, HEAD)
        pltpu.make_async_copy(query.at[:, at], q_all.at[head], load_sem.at[1]).start()
        pltpu.make_async_copy(text.at[:, :, at], mine.at[head], load_sem.at[2]).start()
    for head in range(HEADS):
        at = pl.ds(head * HEAD, HEAD)
        pltpu.make_async_copy(fresh_key.at[:, at], k_all.at[head], load_sem.at[3]).start()
        pltpu.make_async_copy(fresh_value.at[:, at], v_all.at[head], load_sem.at[4]).start()
    loads = [
        pltpu.make_async_copy(target, target, load_sem.at[i])
        for i, target in enumerate((stale_all, q_all, mine, k_all, v_all))
    ]

    partner_low = column * 4 + (1 - low) * 2 + core
    sibling = space + 1 - 2 * core
    barrier = pltpu.get_barrier_semaphore()
    for d in (0, 1):
        @pl.when(has_time[d])
        def _():
            pl.semaphore_signal(barrier, inc=1, device_id={"tm": time - 1 + 2 * d}, device_id_type=MESH)

        @pl.when(has_space[d])
        def _():
            pl.semaphore_signal(barrier, inc=1, device_id={"space": space - 1 + 2 * d}, device_id_type=MESH)

    partners = [partner_low] + [lax.rem(space + 4 * d, spaces) for d in (1, 2, 3)]
    for partner in partners:
        pl.semaphore_signal(barrier, inc=1, device_id={"space": partner}, device_id_type=MESH)

    @pl.when(jnp.logical_or(outer, inner))
    def _():
        for place_at in (0, 1):
            partner = jnp.where(outer, middle - 1 + place_at, place_at * (times - 1))
            pl.semaphore_signal(barrier, inc=1, device_id={"tm": partner}, device_id_type=MESH)

    greeted = len(partners) + sum(has.astype(jnp.int32) for has in has_time + has_space)
    greeted = greeted + 2 * jnp.logical_or(outer, inner).astype(jnp.int32)

    counts = [jnp.int32(0)] * 4
    slots = []
    for head in range(HEADS):
        reach_time, reach_space = window[head, 0], window[head, 1]
        both = reach_time * reach_space
        hits = [both, reach_time - both, reach_space - both, 1 - reach_time - reach_space + both]
        slot = jnp.int32(0)
        for k in range(4):
            slot = slot + hits[k] * (GROUP * k + counts[k])
            counts[k] = counts[k] + hits[k]
        slots.append(slot)
        place[head] = jnp.minimum(slot, HEADS - 1)
    for s in range(HEADS):
        chosen = jnp.int32(0)
        for head in range(HEADS):
            apart = jnp.maximum(slots[head] - s, s - slots[head])
            chosen = chosen + head * jnp.maximum(1 - apart, 0)
        order[s] = chosen

    def pack(target, base):
        for g in range(GROUP):
            target[:, g] = stale_all[order[base + g]]

    def along_time(kind, d, source, target):
        return pltpu.make_async_remote_copy(
            src_ref=source, dst_ref=target.at[1 - d],
            send_sem=send_sem.at[kind, d], recv_sem=recv_sem.at[kind, 1 - d],
            device_id={"tm": time - 1 + 2 * d}, device_id_type=MESH,
        )

    def along_space(kind, d, source, target):
        return pltpu.make_async_remote_copy(
            src_ref=source, dst_ref=target.at[1 - d],
            send_sem=send_sem.at[kind, d], recv_sem=recv_sem.at[kind, 1 - d],
            device_id={"space": space - 1 + 2 * d}, device_id_type=MESH,
        )

    def send_both(has, make, kind, source, target):
        for d in (0, 1):
            @pl.when(has[d])
            def _():
                make(kind, d, source, target).start()

    def arrived(has, make, kind, source, target):
        for d in (0, 1):
            @pl.when(has[d])
            def _():
                make(kind, 1 - d, source, target).wait_recv()

    def sent(has, make, kind, source, target):
        for d in (0, 1):
            @pl.when(has[d])
            def _():
                make(kind, d, source, target).wait_send()

    loads[0].wait()
    pack(pack11, 0)
    pl.semaphore_wait(barrier, greeted)
    send_both(has_time, along_time, 0, pack11, got11)
    loads[2].wait()
    swap = pltpu.make_async_remote_copy(
        src_ref=mine, dst_ref=mine, send_sem=text_send.at[0], recv_sem=text_recv.at[0],
        device_id={"space": partner_low}, device_id_type=MESH,
    )
    swap.start()
    loads[1].wait()
    for g in range(GROUP):
        packq[g] = q_all[order[g]]
    send_both(has_space, along_space, 3, packq, gotq)
    pack(pack01, 2 * GROUP)
    send_both(has_space, along_space, 2, pack01, got01)
    pack(pack10, GROUP)

    pieces = [(kv, g) for g in range(GROUP) for kv in range(2)]

    def detour(d, i):
        kv, g = pieces[i]
        return pltpu.make_async_remote_copy(
            src_ref=pack10.at[kv, g], dst_ref=relay.at[kv, g],
            send_sem=send_sem.at[1, d], recv_sem=relay_recv.at[i],
            device_id={"tm": (times - 1) * (1 - d)}, device_id_type=MESH,
        )

    def onward(d, i):
        kv, g = pieces[i]
        return pltpu.make_async_remote_copy(
            src_ref=relay.at[kv, g], dst_ref=got10.at[1 - d, kv, g],
            send_sem=relay_send, recv_sem=recv_sem.at[1, 1 - d],
            device_id={"tm": middle - 1 + d}, device_id_type=MESH,
        )

    for d in (0, 1):
        @pl.when(bent[d])
        def _():
            for i in range(len(pieces)):
                detour(d, i).start()

    spread = [
        pltpu.make_async_remote_copy(
            src_ref=words.at[core, column], dst_ref=words.at[core, column],
            send_sem=text_send.at[d], recv_sem=text_recv.at[d],
            device_id={"space": lax.rem(space + 4 * d, spaces)}, device_id_type=MESH,
        )
        for d in (1, 2, 3)
    ]

    def rows_at(block):
        return pl.ds(block * ROW_BLOCK, ROW_BLOCK)

    def attend(jobs):
        for job in jobs:
            job["keys"] = jnp.concatenate([chunk[0] for chunk in job["chunks"]], axis=0)
            values = jnp.concatenate([chunk[1] for chunk in job["chunks"]], axis=0)
            ones = jnp.ones((values.shape[0], LANES), jnp.bfloat16)
            job["values"] = jnp.concatenate([values, ones], axis=1)
        tasks = [dict(job, here=rows_at(block)) for job in jobs for block in range(rows // ROW_BLOCK)]

        def score(task):
            query_rows = task["query"](task["here"])
            task["scores"] = lax.dot_general(
                query_rows, task["keys"], (((1,), (1,)), ((), ())),
                preferred_element_type=jnp.float32,
            ) * scale

        def weigh(task):
            pieces, tops, at = [], [], 0
            before = task["before"](task["here"]) if task["before"] else None
            for keys, _, live, valid in task["chunks"]:
                piece = task["scores"][:, at : at + keys.shape[0]]
                at += keys.shape[0]
                if live is not None:
                    piece = jnp.where(live, piece, -1e30)
                top = jnp.broadcast_to(jnp.max(piece, axis=1, keepdims=True), (ROW_BLOCK, LANES))
                if valid is not None:
                    top = jnp.where(valid, top, -1e30)
                pieces.append(piece)
                tops.append(top)
            top = functools.reduce(jnp.maximum, tops + ([before[0]] if before else []))
            weights = []
            for piece, (_, _, _, valid) in zip(pieces, task["chunks"]):
                base = top if valid is None else jnp.where(valid, top, 1e30)
                base = jnp.concatenate([base] * (piece.shape[1] // LANES), axis=1)
                weights.append(jnp.exp2(piece - base).astype(jnp.bfloat16))
            both = jnp.dot(
                jnp.concatenate(weights, axis=1), task["values"], preferred_element_type=jnp.float32
            )
            mixed, total = both[:, :HEAD], both[:, HEAD:]
            if before:
                shrink = jnp.exp2(before[0] - top)
                total = before[1] * shrink + total
                mixed = before[2] * shrink + mixed
            task["after"](task["here"], top, total, mixed)

        score(tasks[0])
        for i, task in enumerate(tasks):
            if i + 1 < len(tasks):
                score(tasks[i + 1])
            weigh(task)

    def job(query, chunks, after, before=None):
        return {"query": query, "chunks": chunks, "before": before, "after": after}

    def own(slot):
        head = order[slot]
        return lambda here: q_all[head, here]

    def saved(g, state):
        return lambda here: (peak[g][state, here], total[g][state, here], mixed[g][state, here])

    def save(g, state):
        def after(here, top, weight, value):
            peak[g][state, here] = top
            total[g][state, here] = weight
            mixed[g][state, here] = value

        return after

    def finish(target, at):
        def after(here, top, weight, value):
            target[(*at, here)] = (value / weight).astype(jnp.bfloat16)

        return after

    def fresh(slot):
        head = order[slot]
        return k_all[head], v_all[head], None, None

    def spoken(slot):
        head = order[slot]
        keys = words[:, :, :, head, 0].reshape(count, HEAD)
        values = words[:, :, :, head, 1].reshape(count, HEAD)
        return keys, values, live, None

    def near(got, g, has):
        return [(got[e, 0, g], got[e, 1, g], None, has[e]) for e in (0, 1)]

    def side_ok(d, position, count):
        return jnp.where(d == 0, position > 0, position < count - 1)

    count = 2 * spaces // 2 * words.shape[5]
    index = lax.broadcasted_iota(jnp.int32, (1, count), 1)
    token = (((index // 32) % 4) * 4 + ((index // 16) % 2) * 2 + index // 128) * 16 + index % 16
    live = token < text_len[0]

    for d in (0, 1):
        @pl.when(jnp.logical_not(has_time[d]))
        def _():
            got11[d] = jnp.zeros_like(got11[d])
            got10[d] = jnp.zeros_like(got10[d])

        @pl.when(jnp.logical_not(has_space[d]))
        def _():
            got01[d] = jnp.zeros_like(got01[d])

    loads[3].wait()
    loads[4].wait()

    @pl.loop(0, 3)
    def _(kind):
        attend([
            job(own(kind * GROUP + g), [fresh(kind * GROUP + g)], save(g, kind))
            for g in range(GROUP)
        ])

    swap.wait_recv()
    for copy in spread:
        copy.start()

    arrived(has_space, along_space, 3, packq, gotq)

    def visitor(d, g):
        return lambda here: gotq[d, g, here]

    @pl.loop(0, 2)
    def _(d):
        @pl.when(side_ok(d, space, spaces))
        def _():
            attend([
                job(visitor(d, g), [(pack11[0, g], pack11[1, g], None, None)], save(g, 3 + d))
                for g in range(GROUP)
            ])

    for d in (0, 1):
        @pl.when(straight[d])
        def _():
            along_time(0, d, pack11, got11).wait_send()
            along_time(1, d, pack10, got10).start()

    for d, relaying in ((1, first), (0, last)):
        @pl.when(relaying)
        def _():
            for i in range(len(pieces)):
                detour(d, i).wait_recv()
                onward(d, i).start()

    arrived(has_time, along_time, 0, pack11, got11)
    lane = lax.broadcasted_iota(jnp.int32, (rows, LANES), 1)

    @pl.loop(0, 2)
    def _(i):
        d = lax.rem(i + core, 2)

        @pl.when(side_ok(d, space, spaces))
        def _():
            def give(g):
                def after(here, top, weight, value):
                    o_send[d, g, here] = (value / weight).astype(jnp.bfloat16)
                    peak[g][3 + d, here] = top + jnp.log2(weight)

                return after

            attend([
                job(visitor(d, g), near(got11, g, has_time), give(g), saved(g, 3 + d))
                for g in range(GROUP)
            ])
            stats = jnp.zeros((rows, LANES), jnp.float32)
            for g in range(GROUP):
                stats = jnp.where(lane == g, peak[g][3 + d], stats)
            o_stat[d] = stats.T[:8]
            along_space(4, d, o_send.at[d], o_got).start()
            along_space(5, d, o_stat.at[d], o_got_stat).start()

    for copy in spread:
        copy.wait_recv()
    half = words.at[core]
    across = pltpu.make_async_remote_copy(
        src_ref=half, dst_ref=half, send_sem=text_send.at[4], recv_sem=text_recv.at[4],
        device_id={"space": sibling}, device_id_type=MESH,
    )
    across.start()
    across.wait_recv()
    attend([
        job(own(3 * GROUP + g), [fresh(3 * GROUP + g), spoken(3 * GROUP + g)], finish(done, (3 * GROUP + g,)))
        for g in range(GROUP)
    ])

    attend([
        job(own(g), [spoken(g), *near(got11, g, has_time)], save(g, 0), saved(g, 0))
        for g in range(GROUP)
    ])
    arrived(has_space, along_space, 2, pack01, got01)
    attend([
        job(own(2 * GROUP + g), [spoken(2 * GROUP + g), *near(got01, g, has_space)], finish(done, (2 * GROUP + g,)), saved(g, 2))
        for g in range(GROUP)
    ])
    arrived(has_time, along_time, 1, pack10, got10)
    attend([
        job(own(GROUP + g), [spoken(GROUP + g), *near(got10, g, has_time)], finish(done, (GROUP + g,)), saved(g, 1))
        for g in range(GROUP)
    ])

    for d in (0, 1):
        @pl.when(has_space[d])
        def _():
            along_space(4, 1 - d, o_send.at[1 - d], o_got).wait_recv()
            along_space(5, 1 - d, o_stat.at[1 - d], o_got_stat).wait_recv()
            spare = jnp.zeros((LANES - 8, rows), jnp.float32)
            stats = jnp.concatenate([o_got_stat[d], spare], axis=0).T
            for g in range(GROUP):
                other = jnp.broadcast_to(stats[:, g : g + 1], (rows, LANES))
                before = peak[g][0]
                top = jnp.maximum(before, other)
                keep = jnp.exp2(before - top)
                add = jnp.exp2(other - top)
                peak[g][0] = top
                mixed[g][0] = mixed[g][0] * keep + o_got[d, g].astype(jnp.float32) * add
                total[g][0] = total[g][0] * keep + add

    for g in range(GROUP):
        done[g] = (mixed[g][0] / total[g][0]).astype(jnp.bfloat16)
    for head in range(HEADS):
        out_all[:, head * HEAD : (head + 1) * HEAD] = done[place[head]]
    store = pltpu.make_async_copy(out_all, out, load_sem.at[5])
    store.start()

    for d in (0, 1):
        @pl.when(bent[d])
        def _():
            along_time(0, d, pack11, got11).wait_send()

    sent(has_time, along_time, 1, pack10, got10)

    @pl.when(outer)
    def _():
        pltpu.make_async_copy(relay, relay, relay_send).wait()

    sent(has_space, along_space, 2, pack01, got01)
    sent(has_space, along_space, 3, packq, gotq)
    for d in (0, 1):
        @pl.when(has_space[d])
        def _():
            along_space(4, d, o_send.at[d], o_got).wait_send()
            along_space(5, d, o_stat.at[d], o_got_stat).wait_send()
    swap.wait_send()
    for copy in spread:
        copy.wait_send()
    across.wait_send()
    store.wait()


def on_device(query, fresh_key, fresh_value, stale_kv, text_kv, window, text_len):
    rows, width = query.shape[2:]
    words = text_kv.shape[1]
    bf16, f32 = jnp.bfloat16, jnp.float32
    heads = (GROUP, rows, HEAD)
    anywhere = pl.BlockSpec(memory_space=pl.ANY)
    scalars = pl.BlockSpec(memory_space=pltpu.SMEM)
    result = pl.pallas_call(
        kernel,
        out_shape=jax.ShapeDtypeStruct((rows, width), bf16),
        in_specs=[anywhere] * 5 + [scalars] * 2,
        out_specs=anywhere,
        scratch_shapes=[
            pltpu.VMEM((HEADS, rows, HEAD), bf16),
            pltpu.VMEM((HEADS, rows, HEAD), bf16),
            pltpu.VMEM((HEADS, rows, HEAD), bf16),
            pltpu.VMEM((HEADS, 2, rows, HEAD), bf16),
            pltpu.VMEM((2, 4, 2, HEADS, 2, words, HEAD), bf16),
            pltpu.VMEM((rows, width), bf16),
            pltpu.VMEM((2, *heads), bf16),
            pltpu.VMEM((2, *heads), bf16),
            pltpu.VMEM((2, *heads), bf16),
            pltpu.VMEM(heads, bf16),
            pltpu.VMEM((2, 2, *heads), bf16),
            pltpu.VMEM((2, 2, *heads), bf16),
            pltpu.VMEM((2, 2, *heads), bf16),
            pltpu.VMEM((2, *heads), bf16),
            pltpu.VMEM((2, *heads), bf16),
            pltpu.VMEM((2, 8, rows), f32),
            pltpu.VMEM((2, *heads), bf16),
            pltpu.VMEM((2, 8, rows), f32),
            [pltpu.VMEM((5, rows, LANES), f32)] * GROUP,
            [pltpu.VMEM((5, rows, LANES), f32)] * GROUP,
            [pltpu.VMEM((5, rows, HEAD), f32)] * GROUP,
            pltpu.VMEM((HEADS, rows, HEAD), bf16),
            pltpu.SMEM((HEADS,), jnp.int32),
            pltpu.SMEM((HEADS,), jnp.int32),
            pltpu.VMEM((2, *heads), bf16),
            pltpu.SemaphoreType.DMA((6,)),
            pltpu.SemaphoreType.DMA((6, 2)),
            pltpu.SemaphoreType.DMA((6, 2)),
            pltpu.SemaphoreType.DMA((5,)),
            pltpu.SemaphoreType.DMA((5,)),
            pltpu.SemaphoreType.DMA(()),
            pltpu.SemaphoreType.DMA((2 * GROUP,)),
        ],
        compiler_params=pltpu.CompilerParams(
            collective_id=0, has_side_effects=True, vmem_limit_bytes=60 << 20
        ),
    )(
        query[0, 0], fresh_key[0, 0], fresh_value[0, 0], stale_kv[:, 0, 0], text_kv,
        window, text_len,
    )
    return result[None, None]


def solution(mesh):
    in_specs = (
        P("tm", "space", None, None),
        P("tm", "space", None, None),
        P("tm", "space", None, None),
        P(None, "tm", "space", None, None),
        P(None, "space", None),
        P(),
        P(),
    )
    out_specs = P("tm", "space", None, None)
    return jax.shard_map(
        on_device, mesh=mesh, in_specs=in_specs, out_specs=out_specs, check_vma=False
    )
```

```python
import functools
import math

import jax
import jax.numpy as jnp
from jax import lax
from jax.experimental import pallas as pl
from jax.experimental.pallas import tpu as pltpu
from jax.sharding import PartitionSpec as P

MESH = pl.DeviceIdType.MESH
HEAD = 128
GROUP = 3
HEADS = 12
LANES = 128
ROW_BLOCK = 384


def slots_of(window):
    counts = [jnp.int32(0)] * 4
    slots = []
    for head in range(HEADS):
        reach_time, reach_space = window[0, head], window[1, head]
        both = reach_time * reach_space
        hits = [both, reach_time - both, reach_space - both, 1 - reach_time - reach_space + both]
        slot = jnp.int32(0)
        for k in range(4):
            slot = slot + hits[k] * (GROUP * k + counts[k])
            counts[k] = counts[k] + hits[k]
        slots.append(slot)
    return slots


def arrange(by_slot, window, out, sems):
    copies = [
        pltpu.make_async_copy(
            by_slot.at[jnp.minimum(slot, HEADS - 1)], out.at[:, pl.ds(head * HEAD, HEAD)], sems.at[head]
        )
        for head, slot in enumerate(slots_of(window))
    ]
    for copy in copies:
        copy.start()
    for copy in copies:
        copy.wait()


def kernel(
    query, fresh_key, fresh_value, stale, text, window, text_len, out,
    q_all, k_all, v_all, stale_all, words,
    pack11, pack10, pack01, packq,
    got11, got10, got01, gotq,
    o_send, o_stat, o_got, o_got_stat,
    peak, total, mixed, done, order,
    relay, load_sem, send_sem, recv_sem, text_send, text_recv, relay_send, relay_recv, store_sem,
):
    rows = q_all.shape[1]
    times = lax.axis_size("tm")
    spaces = lax.axis_size("space")
    time = lax.axis_index("tm")
    space = lax.axis_index("space")
    core = lax.rem(space, 2)
    low = lax.rem(space // 2, 2)
    column = space // 4
    has_time = (time > 0, time < times - 1)
    has_space = (space > 0, space < spaces - 1)
    next_time = (time - 1, time + 1)
    next_space = (space - 1, space + 1)
    middle = times // 2
    first, last = time == 0, time == times - 1
    outer = jnp.logical_or(first, last)
    inner = jnp.logical_or(time == middle - 1, time == middle)
    straight = (
        jnp.logical_and(has_time[0], time != middle),
        jnp.logical_and(has_time[1], time != middle - 1),
    )
    bent = (time == middle, time == middle - 1)
    scale = math.log2(math.e) / math.sqrt(HEAD)

    mine = words.at[core, column, low]
    for head in range(HEADS):
        at = pl.ds(head * HEAD, HEAD)
        pltpu.make_async_copy(stale.at[:, :, at], stale_all.at[head], load_sem.at[0]).start()
    for head in range(HEADS):
        at = pl.ds(head * HEAD, HEAD)
        pltpu.make_async_copy(query.at[:, at], q_all.at[head], load_sem.at[1]).start()
        pltpu.make_async_copy(text.at[:, :, at], mine.at[head], load_sem.at[2]).start()
    for head in range(HEADS):
        at = pl.ds(head * HEAD, HEAD)
        pltpu.make_async_copy(fresh_key.at[:, at], k_all.at[head], load_sem.at[3]).start()
        pltpu.make_async_copy(fresh_value.at[:, at], v_all.at[head], load_sem.at[4]).start()
    loads = [
        pltpu.make_async_copy(target, target, load_sem.at[i])
        for i, target in enumerate((stale_all, q_all, mine, k_all, v_all))
    ]

    partner_low = column * 4 + (1 - low) * 2 + core
    sibling = space + 1 - 2 * core
    barrier = pltpu.get_barrier_semaphore()
    for d in (0, 1):
        @pl.when(has_time[d])
        def _():
            pl.semaphore_signal(barrier, inc=1, device_id={"tm": time - 1 + 2 * d}, device_id_type=MESH)

        @pl.when(has_space[d])
        def _():
            pl.semaphore_signal(barrier, inc=1, device_id={"space": space - 1 + 2 * d}, device_id_type=MESH)

    partners = [partner_low] + [lax.rem(space + 4 * d, spaces) for d in (1, 2, 3)]
    for partner in partners:
        pl.semaphore_signal(barrier, inc=1, device_id={"space": partner}, device_id_type=MESH)

    @pl.when(jnp.logical_or(outer, inner))
    def _():
        for place_at in (0, 1):
            partner = jnp.where(outer, middle - 1 + place_at, place_at * (times - 1))
            pl.semaphore_signal(barrier, inc=1, device_id={"tm": partner}, device_id_type=MESH)

    greeted = len(partners) + sum(has.astype(jnp.int32) for has in has_time + has_space)
    greeted = greeted + 2 * jnp.logical_or(outer, inner).astype(jnp.int32)

    slots = slots_of(window)
    for s in range(HEADS):
        chosen = jnp.int32(0)
        for head in range(HEADS):
            apart = jnp.maximum(slots[head] - s, s - slots[head])
            chosen = chosen + head * jnp.maximum(1 - apart, 0)
        order[s] = chosen

    def pack(target, base):
        for g in range(GROUP):
            target[:, g] = stale_all[order[base + g]]

    def along_time(kind, d, source, target):
        return pltpu.make_async_remote_copy(
            src_ref=source, dst_ref=target.at[1 - d],
            send_sem=send_sem.at[kind, d], recv_sem=recv_sem.at[kind, 1 - d],
            device_id={"tm": time - 1 + 2 * d}, device_id_type=MESH,
        )

    def along_space(kind, d, source, target):
        return pltpu.make_async_remote_copy(
            src_ref=source, dst_ref=target.at[1 - d],
            send_sem=send_sem.at[kind, d], recv_sem=recv_sem.at[kind, 1 - d],
            device_id={"space": space - 1 + 2 * d}, device_id_type=MESH,
        )

    def send_both(has, make, kind, source, target):
        for d in (0, 1):
            @pl.when(has[d])
            def _():
                make(kind, d, source, target).start()

    def arrived(has, make, kind, source, target):
        for d in (0, 1):
            @pl.when(has[d])
            def _():
                make(kind, 1 - d, source, target).wait_recv()

    def sent(has, make, kind, source, target):
        for d in (0, 1):
            @pl.when(has[d])
            def _():
                make(kind, d, source, target).wait_send()

    loads[0].wait()
    pack(pack11, 0)
    pl.semaphore_wait(barrier, greeted)
    send_both(has_time, along_time, 0, pack11, got11)
    loads[2].wait()
    swap = pltpu.make_async_remote_copy(
        src_ref=mine, dst_ref=mine, send_sem=text_send.at[0], recv_sem=text_recv.at[0],
        device_id={"space": partner_low}, device_id_type=MESH,
    )
    swap.start()
    loads[1].wait()
    for g in range(GROUP):
        packq[g] = q_all[order[g]]
    send_both(has_space, along_space, 3, packq, gotq)
    pack(pack01, 2 * GROUP)
    pack(pack10, GROUP)

    pieces = [(kv, g) for g in range(GROUP) for kv in range(2)]

    def detour(d, i):
        kv, g = pieces[i]
        return pltpu.make_async_remote_copy(
            src_ref=pack10.at[kv, g], dst_ref=relay.at[kv, g],
            send_sem=send_sem.at[1, d], recv_sem=relay_recv.at[i],
            device_id={"tm": (times - 1) * (1 - d)}, device_id_type=MESH,
        )

    def onward(d, i):
        kv, g = pieces[i]
        return pltpu.make_async_remote_copy(
            src_ref=relay.at[kv, g], dst_ref=got10.at[1 - d, kv, g],
            send_sem=relay_send, recv_sem=recv_sem.at[1, 1 - d],
            device_id={"tm": middle - 1 + d}, device_id_type=MESH,
        )

    for d in (0, 1):
        @pl.when(bent[d])
        def _():
            for i in range(len(pieces)):
                detour(d, i).start()

    spread = [
        pltpu.make_async_remote_copy(
            src_ref=words.at[core, column], dst_ref=words.at[core, column],
            send_sem=text_send.at[d], recv_sem=text_recv.at[d],
            device_id={"space": lax.rem(space + 4 * d, spaces)}, device_id_type=MESH,
        )
        for d in (1, 2, 3)
    ]

    def stored(kind):
        here = pl.ds(kind * GROUP, GROUP)
        return pltpu.make_async_copy(done.at[here], out.at[here], store_sem.at[kind])

    def store_kind(kind):
        stored(kind).start()

    def rows_at(block):
        return pl.ds(block * ROW_BLOCK, ROW_BLOCK)

    def attend(jobs):
        for job in jobs:
            job["keys"] = jnp.concatenate([chunk[0] for chunk in job["chunks"]], axis=0)
            values = jnp.concatenate([chunk[1] for chunk in job["chunks"]], axis=0)
            ones = jnp.ones((values.shape[0], LANES), jnp.bfloat16)
            job["values"] = jnp.concatenate([values, ones], axis=1)
        tasks = [dict(job, here=rows_at(block)) for job in jobs for block in range(rows // ROW_BLOCK)]

        def score(task):
            query_rows = task["query"](task["here"])
            task["scores"] = lax.dot_general(
                query_rows, task["keys"], (((1,), (1,)), ((), ())),
                preferred_element_type=jnp.float32,
            ) * scale

        def weigh(task):
            pieces, tops, at = [], [], 0
            before = task["before"](task["here"]) if task["before"] else None
            for keys, _, live, valid in task["chunks"]:
                piece = task["scores"][:, at : at + keys.shape[0]]
                at += keys.shape[0]
                if live is not None:
                    piece = jnp.where(live, piece, -1e30)
                top = jnp.broadcast_to(jnp.max(piece, axis=1, keepdims=True), (ROW_BLOCK, LANES))
                if valid is not None:
                    top = jnp.where(valid, top, -1e30)
                pieces.append(piece)
                tops.append(top)
            top = functools.reduce(jnp.maximum, tops + ([before[0]] if before else []))
            weights = []
            for piece, (_, _, _, valid) in zip(pieces, task["chunks"]):
                base = top if valid is None else jnp.where(valid, top, 1e30)
                base = jnp.concatenate([base] * (piece.shape[1] // LANES), axis=1)
                weights.append(jnp.exp2(piece - base).astype(jnp.bfloat16))
            both = jnp.dot(
                jnp.concatenate(weights, axis=1), task["values"], preferred_element_type=jnp.float32
            )
            mixed, total = both[:, :HEAD], both[:, HEAD:]
            if before:
                shrink = jnp.exp2(before[0] - top)
                total = before[1] * shrink + total
                mixed = before[2] * shrink + mixed
            task["after"](task["here"], top, total, mixed)

        score(tasks[0])
        for i, task in enumerate(tasks):
            if i + 1 < len(tasks):
                score(tasks[i + 1])
            weigh(task)

    def job(query, chunks, after, before=None):
        return {"query": query, "chunks": chunks, "before": before, "after": after}

    def own(slot):
        head = order[slot]
        return lambda here: q_all[head, here]

    def saved(g, state):
        return lambda here: (peak[g][state, here], total[g][state, here], mixed[g][state, here])

    def save(g, state):
        def after(here, top, weight, value):
            peak[g][state, here] = top
            total[g][state, here] = weight
            mixed[g][state, here] = value

        return after

    def finish(target, at):
        def after(here, top, weight, value):
            target[(*at, here)] = (value / weight).astype(jnp.bfloat16)

        return after

    def fresh(slot):
        head = order[slot]
        return k_all[head], v_all[head], None, None

    def spoken(slot):
        head = order[slot]
        keys = words[:, :, :, head, 0].reshape(count, HEAD)
        values = words[:, :, :, head, 1].reshape(count, HEAD)
        return keys, values, live, None

    def near(got, g, has):
        return [(got[e, 0, g], got[e, 1, g], None, has[e]) for e in (0, 1)]

    def side_ok(d, position, count):
        return jnp.where(d == 0, position > 0, position < count - 1)

    count = 2 * spaces // 2 * words.shape[5]
    index = lax.broadcasted_iota(jnp.int32, (1, count), 1)
    token = (((index // 32) % 4) * 4 + ((index // 16) % 2) * 2 + index // 128) * 16 + index % 16
    live = token < text_len[0]

    for d in (0, 1):
        @pl.when(jnp.logical_not(has_time[d]))
        def _():
            got11[d] = jnp.zeros_like(got11[d])
            got10[d] = jnp.zeros_like(got10[d])

        @pl.when(jnp.logical_not(has_space[d]))
        def _():
            got01[d] = jnp.zeros_like(got01[d])

    loads[3].wait()
    loads[4].wait()

    @pl.loop(0, 3)
    def _(kind):
        attend([
            job(own(kind * GROUP + g), [fresh(kind * GROUP + g)], save(g, kind))
            for g in range(GROUP)
        ])

    swap.wait_recv()
    for copy in spread:
        copy.start()

    arrived(has_space, along_space, 3, packq, gotq)

    def visitor(d, g):
        return lambda here: gotq[d, g, here]

    @pl.loop(0, 2)
    def _(d):
        @pl.when(side_ok(d, space, spaces))
        def _():
            attend([
                job(visitor(d, g), [(pack11[0, g], pack11[1, g], None, None)], save(g, 3 + d))
                for g in range(GROUP)
            ])

    def send_sides():
        send_both(has_space, along_space, 2, pack01, got01)

    pl.when(jnp.logical_not(outer))(send_sides)

    for d in (0, 1):
        @pl.when(straight[d])
        def _():
            along_time(0, d, pack11, got11).wait_send()
            along_time(1, d, pack10, got10).start()

    for d, relaying in ((1, first), (0, last)):
        @pl.when(relaying)
        def _():
            for i in range(len(pieces)):
                detour(d, i).wait_recv()
                onward(d, i).start()

    arrived(has_time, along_time, 0, pack11, got11)
    lane = lax.broadcasted_iota(jnp.int32, (rows, LANES), 1)

    @pl.loop(0, 2)
    def _(i):
        d = lax.rem(i + core, 2)

        @pl.when(side_ok(d, space, spaces))
        def _():
            def give(g):
                def after(here, top, weight, value):
                    o_send[d, g, here] = (value / weight).astype(jnp.bfloat16)
                    peak[g][3 + d, here] = top + jnp.log2(weight)

                return after

            attend([
                job(visitor(d, g), near(got11, g, has_time), give(g), saved(g, 3 + d))
                for g in range(GROUP)
            ])
            stats = jnp.zeros((rows, LANES), jnp.float32)
            for g in range(GROUP):
                stats = jnp.where(lane == g, peak[g][3 + d], stats)
            o_stat[d] = stats.T[:8]
            along_space(4, d, o_send.at[d], o_got).start()
            along_space(5, d, o_stat.at[d], o_got_stat).start()

    pl.when(outer)(send_sides)

    for copy in spread:
        copy.wait_recv()
    half = words.at[core]
    across = pltpu.make_async_remote_copy(
        src_ref=half, dst_ref=half, send_sem=text_send.at[4], recv_sem=text_recv.at[4],
        device_id={"space": sibling}, device_id_type=MESH,
    )
    across.start()
    across.wait_recv()
    attend([
        job(own(3 * GROUP + g), [fresh(3 * GROUP + g), spoken(3 * GROUP + g)], finish(done, (3 * GROUP + g,)))
        for g in range(GROUP)
    ])
    store_kind(3)

    attend([
        job(own(g), [spoken(g), *near(got11, g, has_time)], save(g, 0), saved(g, 0))
        for g in range(GROUP)
    ])
    arrived(has_space, along_space, 2, pack01, got01)
    attend([
        job(own(2 * GROUP + g), [spoken(2 * GROUP + g), *near(got01, g, has_space)], finish(done, (2 * GROUP + g,)), saved(g, 2))
        for g in range(GROUP)
    ])
    store_kind(2)
    arrived(has_time, along_time, 1, pack10, got10)
    attend([
        job(own(GROUP + g), [spoken(GROUP + g), *near(got10, g, has_time)], finish(done, (GROUP + g,)), saved(g, 1))
        for g in range(GROUP)
    ])
    store_kind(1)

    for d in (0, 1):
        @pl.when(has_space[d])
        def _():
            along_space(4, 1 - d, o_send.at[1 - d], o_got).wait_recv()
            along_space(5, 1 - d, o_stat.at[1 - d], o_got_stat).wait_recv()
            spare = jnp.zeros((LANES - 8, rows), jnp.float32)
            stats = jnp.concatenate([o_got_stat[d], spare], axis=0).T
            for g in range(GROUP):
                other = jnp.broadcast_to(stats[:, g : g + 1], (rows, LANES))
                before = peak[g][0]
                top = jnp.maximum(before, other)
                keep = jnp.exp2(before - top)
                add = jnp.exp2(other - top)
                peak[g][0] = top
                mixed[g][0] = mixed[g][0] * keep + o_got[d, g].astype(jnp.float32) * add
                total[g][0] = total[g][0] * keep + add

    for g in range(GROUP):
        done[g] = (mixed[g][0] / total[g][0]).astype(jnp.bfloat16)
    store_kind(0)

    for d in (0, 1):
        @pl.when(bent[d])
        def _():
            along_time(0, d, pack11, got11).wait_send()

    sent(has_time, along_time, 1, pack10, got10)

    @pl.when(outer)
    def _():
        pltpu.make_async_copy(relay, relay, relay_send).wait()

    sent(has_space, along_space, 2, pack01, got01)
    sent(has_space, along_space, 3, packq, gotq)
    for d in (0, 1):
        @pl.when(has_space[d])
        def _():
            along_space(4, d, o_send.at[d], o_got).wait_send()
            along_space(5, d, o_stat.at[d], o_got_stat).wait_send()
    swap.wait_send()
    for copy in spread:
        copy.wait_send()
    across.wait_send()
    for kind in range(4):
        stored(kind).wait()


def on_device(query, fresh_key, fresh_value, stale_kv, text_kv, window, text_len):
    rows, width = query.shape[2:]
    words = text_kv.shape[1]
    bf16, f32 = jnp.bfloat16, jnp.float32
    heads = (GROUP, rows, HEAD)
    anywhere = pl.BlockSpec(memory_space=pl.ANY)
    scalars = pl.BlockSpec(memory_space=pltpu.SMEM)
    by_slot = pl.pallas_call(
        kernel,
        out_shape=jax.ShapeDtypeStruct((HEADS, rows, HEAD), bf16),
        in_specs=[anywhere] * 5 + [scalars] * 2,
        out_specs=anywhere,
        scratch_shapes=[
            pltpu.VMEM((HEADS, rows, HEAD), bf16),
            pltpu.VMEM((HEADS, rows, HEAD), bf16),
            pltpu.VMEM((HEADS, rows, HEAD), bf16),
            pltpu.VMEM((HEADS, 2, rows, HEAD), bf16),
            pltpu.VMEM((2, 4, 2, HEADS, 2, words, HEAD), bf16),
            pltpu.VMEM((2, *heads), bf16),
            pltpu.VMEM((2, *heads), bf16),
            pltpu.VMEM((2, *heads), bf16),
            pltpu.VMEM(heads, bf16),
            pltpu.VMEM((2, 2, *heads), bf16),
            pltpu.VMEM((2, 2, *heads), bf16),
            pltpu.VMEM((2, 2, *heads), bf16),
            pltpu.VMEM((2, *heads), bf16),
            pltpu.VMEM((2, *heads), bf16),
            pltpu.VMEM((2, 8, rows), f32),
            pltpu.VMEM((2, *heads), bf16),
            pltpu.VMEM((2, 8, rows), f32),
            [pltpu.VMEM((5, rows, LANES), f32)] * GROUP,
            [pltpu.VMEM((5, rows, LANES), f32)] * GROUP,
            [pltpu.VMEM((5, rows, HEAD), f32)] * GROUP,
            pltpu.VMEM((HEADS, rows, HEAD), bf16),
            pltpu.SMEM((HEADS,), jnp.int32),
            pltpu.VMEM((2, *heads), bf16),
            pltpu.SemaphoreType.DMA((5,)),
            pltpu.SemaphoreType.DMA((6, 2)),
            pltpu.SemaphoreType.DMA((6, 2)),
            pltpu.SemaphoreType.DMA((5,)),
            pltpu.SemaphoreType.DMA((5,)),
            pltpu.SemaphoreType.DMA(()),
            pltpu.SemaphoreType.DMA((2 * GROUP,)),
            pltpu.SemaphoreType.DMA((4,)),
        ],
        compiler_params=pltpu.CompilerParams(
            collective_id=0, has_side_effects=True, vmem_limit_bytes=60 << 20
        ),
    )(
        query[0, 0], fresh_key[0, 0], fresh_value[0, 0], stale_kv[:, 0, 0], text_kv,
        window.T, text_len,
    )
    result = pl.pallas_call(
        arrange,
        out_shape=jax.ShapeDtypeStruct((rows, width), bf16),
        in_specs=[anywhere, scalars],
        out_specs=anywhere,
        scratch_shapes=[pltpu.SemaphoreType.DMA((HEADS,))],
        compiler_params=pltpu.CompilerParams(vmem_limit_bytes=60 << 20),
    )(by_slot, window.T)
    return result[None, None]


def solution(mesh):
    in_specs = (
        P("tm", "space", None, None),
        P("tm", "space", None, None),
        P("tm", "space", None, None),
        P(None, "tm", "space", None, None),
        P(None, "space", None),
        P(),
        P(),
    )
    out_specs = P("tm", "space", None, None)
    return jax.shard_map(
        on_device, mesh=mesh, in_specs=in_specs, out_specs=out_specs, check_vma=False
    )
```

```python
import functools
import math

import jax
import jax.numpy as jnp
from jax import lax
from jax.experimental import pallas as pl
from jax.experimental.pallas import tpu as pltpu
from jax.sharding import PartitionSpec as P

MESH = pl.DeviceIdType.MESH
HEAD = 128
GROUP = 3
HEADS = 12
LANES = 128
ROW_BLOCK = 384


def slots_of(window):
    counts = [jnp.int32(0)] * 4
    slots = []
    for head in range(HEADS):
        reach_time, reach_space = window[0, head], window[1, head]
        both = reach_time * reach_space
        hits = [both, reach_time - both, reach_space - both, 1 - reach_time - reach_space + both]
        slot = jnp.int32(0)
        for k in range(4):
            slot = slot + hits[k] * (GROUP * k + counts[k])
            counts[k] = counts[k] + hits[k]
        slots.append(slot)
    return slots


def arrange(by_slot, window, out, staged, load_sem, store_sem):
    loads, stores = [], []
    for head, slot in enumerate(slots_of(window)):
        source = by_slot.at[jnp.minimum(slot, HEADS - 1)]
        target = out.at[:, pl.ds(head * HEAD, HEAD)]
        loads.append(pltpu.make_async_copy(source, staged.at[head], load_sem.at[head]))
        stores.append(pltpu.make_async_copy(staged.at[head], target, store_sem.at[head]))
    for load in loads:
        load.start()
    for load, store in zip(loads, stores):
        load.wait()
        store.start()
    for store in stores:
        store.wait()


def kernel(
    query, fresh_key, fresh_value, stale, text, window, text_len, out,
    q_all, k_all, v_all, stale_all, words,
    pack11, pack10, pack01, packq,
    got11, got10, got01, gotq,
    o_send, o_stat, o_got, o_got_stat,
    peak, total, mixed, done, order,
    relay, load_sem, send_sem, recv_sem, text_send, text_recv, relay_send, relay_recv, store_sem,
):
    rows = q_all.shape[1]
    times = lax.axis_size("tm")
    spaces = lax.axis_size("space")
    time = lax.axis_index("tm")
    space = lax.axis_index("space")
    core = lax.rem(space, 2)
    low = lax.rem(space // 2, 2)
    column = space // 4
    has_time = (time > 0, time < times - 1)
    has_space = (space > 0, space < spaces - 1)
    next_time = (time - 1, time + 1)
    next_space = (space - 1, space + 1)
    middle = times // 2
    inner = jnp.logical_or(time == middle - 1, time == middle)
    straight = (
        jnp.logical_and(has_time[0], time != middle),
        jnp.logical_and(has_time[1], time != middle - 1),
    )
    bent = (time == middle, time == middle - 1)
    scale = math.log2(math.e) / math.sqrt(HEAD)

    mine = words.at[core, column, low]
    for head in range(HEADS):
        at = pl.ds(head * HEAD, HEAD)
        pltpu.make_async_copy(stale.at[:, :, at], stale_all.at[head], load_sem.at[0]).start()
    for head in range(HEADS):
        at = pl.ds(head * HEAD, HEAD)
        pltpu.make_async_copy(query.at[:, at], q_all.at[head], load_sem.at[1]).start()
        pltpu.make_async_copy(text.at[:, :, at], mine.at[head], load_sem.at[2]).start()
    for head in range(HEADS):
        at = pl.ds(head * HEAD, HEAD)
        pltpu.make_async_copy(fresh_key.at[:, at], k_all.at[head], load_sem.at[3]).start()
        pltpu.make_async_copy(fresh_value.at[:, at], v_all.at[head], load_sem.at[4]).start()
    loads = [
        pltpu.make_async_copy(target, target, load_sem.at[i])
        for i, target in enumerate((stale_all, q_all, mine, k_all, v_all))
    ]

    partner_low = column * 4 + (1 - low) * 2 + core
    sibling = space + 1 - 2 * core
    barrier = pltpu.get_barrier_semaphore()
    for d in (0, 1):
        @pl.when(has_time[d])
        def _():
            pl.semaphore_signal(barrier, inc=1, device_id={"tm": time - 1 + 2 * d}, device_id_type=MESH)

        @pl.when(has_space[d])
        def _():
            pl.semaphore_signal(barrier, inc=1, device_id={"space": space - 1 + 2 * d}, device_id_type=MESH)

    partners = [partner_low] + [lax.rem(space + 4 * d, spaces) for d in (1, 2, 3)]
    for partner in partners:
        pl.semaphore_signal(barrier, inc=1, device_id={"space": partner}, device_id_type=MESH)

    @pl.when(inner)
    def _():
        opposite = {"tm": 2 * middle - 1 - time, "space": partner_low}
        pl.semaphore_signal(barrier, inc=1, device_id=opposite, device_id_type=MESH)

    greeted = len(partners) + sum(has.astype(jnp.int32) for has in has_time + has_space)
    greeted = greeted + inner.astype(jnp.int32)

    slots = slots_of(window)
    for s in range(HEADS):
        chosen = jnp.int32(0)
        for head in range(HEADS):
            apart = jnp.maximum(slots[head] - s, s - slots[head])
            chosen = chosen + head * jnp.maximum(1 - apart, 0)
        order[s] = chosen

    def pack(target, base):
        for g in range(GROUP):
            target[:, g] = stale_all[order[base + g]]

    def along_time(kind, d, source, target):
        return pltpu.make_async_remote_copy(
            src_ref=source, dst_ref=target.at[1 - d],
            send_sem=send_sem.at[kind, d], recv_sem=recv_sem.at[kind, 1 - d],
            device_id={"tm": time - 1 + 2 * d}, device_id_type=MESH,
        )

    def along_space(kind, d, source, target):
        return pltpu.make_async_remote_copy(
            src_ref=source, dst_ref=target.at[1 - d],
            send_sem=send_sem.at[kind, d], recv_sem=recv_sem.at[kind, 1 - d],
            device_id={"space": space - 1 + 2 * d}, device_id_type=MESH,
        )

    def send_both(has, make, kind, source, target):
        for d in (0, 1):
            @pl.when(has[d])
            def _():
                make(kind, d, source, target).start()

    def arrived(has, make, kind, source, target):
        for d in (0, 1):
            @pl.when(has[d])
            def _():
                make(kind, 1 - d, source, target).wait_recv()

    def sent(has, make, kind, source, target):
        for d in (0, 1):
            @pl.when(has[d])
            def _():
                make(kind, d, source, target).wait_send()

    loads[0].wait()
    pack(pack11, 0)
    pl.semaphore_wait(barrier, greeted)
    send_both(has_time, along_time, 0, pack11, got11)
    loads[2].wait()
    swap = pltpu.make_async_remote_copy(
        src_ref=mine, dst_ref=mine, send_sem=text_send.at[0], recv_sem=text_recv.at[0],
        device_id={"space": partner_low}, device_id_type=MESH,
    )
    swap.start()
    loads[1].wait()
    for g in range(GROUP):
        packq[g] = q_all[order[g]]
    send_both(has_space, along_space, 3, packq, gotq)
    pack(pack10, GROUP)

    pieces = [(kv, g) for g in range(GROUP) for kv in range(2)]

    def detour(d, i):
        kv, g = pieces[i]
        return pltpu.make_async_remote_copy(
            src_ref=pack10.at[kv, g], dst_ref=relay.at[kv, g],
            send_sem=send_sem.at[1, d], recv_sem=relay_recv.at[i],
            device_id={"space": partner_low}, device_id_type=MESH,
        )

    def onward(d, i):
        kv, g = pieces[i]
        return pltpu.make_async_remote_copy(
            src_ref=relay.at[kv, g], dst_ref=got10.at[1 - d, kv, g],
            send_sem=relay_send, recv_sem=recv_sem.at[1, 1 - d],
            device_id={"tm": time - 1 + 2 * d, "space": partner_low}, device_id_type=MESH,
        )

    for d in (0, 1):
        @pl.when(bent[d])
        def _():
            for i in range(len(pieces)):
                detour(d, i).start()

    pack(pack01, 2 * GROUP)
    send_both(has_space, along_space, 2, pack01, got01)

    spread = [
        pltpu.make_async_remote_copy(
            src_ref=words.at[core, column], dst_ref=words.at[core, column],
            send_sem=text_send.at[d], recv_sem=text_recv.at[d],
            device_id={"space": lax.rem(space + 4 * d, spaces)}, device_id_type=MESH,
        )
        for d in (1, 2, 3)
    ]

    def stored(kind):
        here = pl.ds(kind * GROUP, GROUP)
        return pltpu.make_async_copy(done.at[here], out.at[here], store_sem.at[kind])

    def store_kind(kind):
        stored(kind).start()

    def rows_at(block):
        return pl.ds(block * ROW_BLOCK, ROW_BLOCK)

    def attend(jobs):
        for job in jobs:
            job["keys"] = jnp.concatenate([chunk[0] for chunk in job["chunks"]], axis=0)
            values = jnp.concatenate([chunk[1] for chunk in job["chunks"]], axis=0)
            ones = jnp.ones((values.shape[0], LANES), jnp.bfloat16)
            job["values"] = jnp.concatenate([values, ones], axis=1)
        tasks = [dict(job, here=rows_at(block)) for job in jobs for block in range(rows // ROW_BLOCK)]

        def score(task):
            query_rows = task["query"](task["here"])
            task["scores"] = lax.dot_general(
                query_rows, task["keys"], (((1,), (1,)), ((), ())),
                preferred_element_type=jnp.float32,
            ) * scale

        def weigh(task):
            pieces, tops, at = [], [], 0
            before = task["before"](task["here"]) if task["before"] else None
            for keys, _, live, valid in task["chunks"]:
                piece = task["scores"][:, at : at + keys.shape[0]]
                at += keys.shape[0]
                if live is not None:
                    piece = jnp.where(live, piece, -1e30)
                top = jnp.broadcast_to(jnp.max(piece, axis=1, keepdims=True), (ROW_BLOCK, LANES))
                if valid is not None:
                    top = jnp.where(valid, top, -1e30)
                pieces.append(piece)
                tops.append(top)
            top = functools.reduce(jnp.maximum, tops + ([before[0]] if before else []))
            weights = []
            for piece, (_, _, _, valid) in zip(pieces, task["chunks"]):
                base = top if valid is None else jnp.where(valid, top, 1e30)
                base = jnp.concatenate([base] * (piece.shape[1] // LANES), axis=1)
                weights.append(jnp.exp2(piece - base).astype(jnp.bfloat16))
            both = jnp.dot(
                jnp.concatenate(weights, axis=1), task["values"], preferred_element_type=jnp.float32
            )
            mixed, total = both[:, :HEAD], both[:, HEAD:]
            if before:
                shrink = jnp.exp2(before[0] - top)
                total = before[1] * shrink + total
                mixed = before[2] * shrink + mixed
            task["after"](task["here"], top, total, mixed)

        score(tasks[0])
        for i, task in enumerate(tasks):
            if i + 1 < len(tasks):
                score(tasks[i + 1])
            weigh(task)

    def job(query, chunks, after, before=None):
        return {"query": query, "chunks": chunks, "before": before, "after": after}

    def own(slot):
        head = order[slot]
        return lambda here: q_all[head, here]

    def saved(g, state):
        return lambda here: (peak[g][state, here], total[g][state, here], mixed[g][state, here])

    def save(g, state):
        def after(here, top, weight, value):
            peak[g][state, here] = top
            total[g][state, here] = weight
            mixed[g][state, here] = value

        return after

    def finish(target, at):
        def after(here, top, weight, value):
            target[(*at, here)] = (value / weight).astype(jnp.bfloat16)

        return after

    def fresh(slot):
        head = order[slot]
        return k_all[head], v_all[head], None, None

    def spoken(slot):
        head = order[slot]
        keys = words[:, :, :, head, 0].reshape(count, HEAD)
        values = words[:, :, :, head, 1].reshape(count, HEAD)
        return keys, values, live, None

    def near(got, g, has):
        return [(got[e, 0, g], got[e, 1, g], None, has[e]) for e in (0, 1)]

    def side_ok(d, position, count):
        return jnp.where(d == 0, position > 0, position < count - 1)

    count = 2 * spaces // 2 * words.shape[5]
    index = lax.broadcasted_iota(jnp.int32, (1, count), 1)
    token = (((index // 32) % 4) * 4 + ((index // 16) % 2) * 2 + index // 128) * 16 + index % 16
    live = token < text_len[0]

    for d in (0, 1):
        @pl.when(jnp.logical_not(has_time[d]))
        def _():
            got11[d] = jnp.zeros_like(got11[d])
            got10[d] = jnp.zeros_like(got10[d])

        @pl.when(jnp.logical_not(has_space[d]))
        def _():
            got01[d] = jnp.zeros_like(got01[d])

    loads[3].wait()
    loads[4].wait()

    @pl.loop(0, 3)
    def _(kind):
        attend([
            job(own(kind * GROUP + g), [fresh(kind * GROUP + g)], save(g, kind))
            for g in range(GROUP)
        ])

    swap.wait_recv()
    for copy in spread:
        copy.start()

    arrived(has_space, along_space, 3, packq, gotq)

    def visitor(d, g):
        return lambda here: gotq[d, g, here]

    @pl.loop(0, 2)
    def _(d):
        @pl.when(side_ok(d, space, spaces))
        def _():
            attend([
                job(visitor(d, g), [(pack11[0, g], pack11[1, g], None, None)], save(g, 3 + d))
                for g in range(GROUP)
            ])

    for d in (0, 1):
        @pl.when(straight[d])
        def _():
            along_time(0, d, pack11, got11).wait_send()
            along_time(1, d, pack10, got10).start()

    for d in (0, 1):
        @pl.when(bent[d])
        def _():
            for i in range(len(pieces)):
                detour(d, i).wait_recv()
                onward(d, i).start()

    arrived(has_time, along_time, 0, pack11, got11)
    lane = lax.broadcasted_iota(jnp.int32, (rows, LANES), 1)

    @pl.loop(0, 2)
    def _(i):
        d = lax.rem(i + core, 2)

        @pl.when(side_ok(d, space, spaces))
        def _():
            def give(g):
                def after(here, top, weight, value):
                    o_send[d, g, here] = (value / weight).astype(jnp.bfloat16)
                    peak[g][3 + d, here] = top + jnp.log2(weight)

                return after

            attend([
                job(visitor(d, g), near(got11, g, has_time), give(g), saved(g, 3 + d))
                for g in range(GROUP)
            ])
            stats = jnp.zeros((rows, LANES), jnp.float32)
            for g in range(GROUP):
                stats = jnp.where(lane == g, peak[g][3 + d], stats)
            o_stat[d] = stats.T[:8]
            along_space(4, d, o_send.at[d], o_got).start()
            along_space(5, d, o_stat.at[d], o_got_stat).start()

    for copy in spread:
        copy.wait_recv()
    half = words.at[core]
    across = pltpu.make_async_remote_copy(
        src_ref=half, dst_ref=half, send_sem=text_send.at[4], recv_sem=text_recv.at[4],
        device_id={"space": sibling}, device_id_type=MESH,
    )
    across.start()
    across.wait_recv()
    attend([
        job(own(3 * GROUP + g), [fresh(3 * GROUP + g), spoken(3 * GROUP + g)], finish(done, (3 * GROUP + g,)))
        for g in range(GROUP)
    ])
    store_kind(3)

    attend([
        job(own(g), [spoken(g), *near(got11, g, has_time)], save(g, 0), saved(g, 0))
        for g in range(GROUP)
    ])
    arrived(has_space, along_space, 2, pack01, got01)
    attend([
        job(own(2 * GROUP + g), [spoken(2 * GROUP + g), *near(got01, g, has_space)], finish(done, (2 * GROUP + g,)), saved(g, 2))
        for g in range(GROUP)
    ])
    store_kind(2)
    arrived(has_time, along_time, 1, pack10, got10)
    attend([
        job(own(GROUP + g), [spoken(GROUP + g), *near(got10, g, has_time)], finish(done, (GROUP + g,)), saved(g, 1))
        for g in range(GROUP)
    ])
    store_kind(1)

    for d in (0, 1):
        @pl.when(has_space[d])
        def _():
            along_space(4, 1 - d, o_send.at[1 - d], o_got).wait_recv()
            along_space(5, 1 - d, o_stat.at[1 - d], o_got_stat).wait_recv()
            spare = jnp.zeros((LANES - 8, rows), jnp.float32)
            stats = jnp.concatenate([o_got_stat[d], spare], axis=0).T
            for g in range(GROUP):
                other = jnp.broadcast_to(stats[:, g : g + 1], (rows, LANES))
                before = peak[g][0]
                top = jnp.maximum(before, other)
                keep = jnp.exp2(before - top)
                add = jnp.exp2(other - top)
                peak[g][0] = top
                mixed[g][0] = mixed[g][0] * keep + o_got[d, g].astype(jnp.float32) * add
                total[g][0] = total[g][0] * keep + add

    for g in range(GROUP):
        done[g] = (mixed[g][0] / total[g][0]).astype(jnp.bfloat16)
    store_kind(0)

    for d in (0, 1):
        @pl.when(bent[d])
        def _():
            along_time(0, d, pack11, got11).wait_send()

    sent(has_time, along_time, 1, pack10, got10)

    @pl.when(inner)
    def _():
        pltpu.make_async_copy(relay, relay, relay_send).wait()

    sent(has_space, along_space, 2, pack01, got01)
    sent(has_space, along_space, 3, packq, gotq)
    for d in (0, 1):
        @pl.when(has_space[d])
        def _():
            along_space(4, d, o_send.at[d], o_got).wait_send()
            along_space(5, d, o_stat.at[d], o_got_stat).wait_send()
    swap.wait_send()
    for copy in spread:
        copy.wait_send()
    across.wait_send()
    for kind in range(4):
        stored(kind).wait()


def on_device(query, fresh_key, fresh_value, stale_kv, text_kv, window, text_len):
    rows, width = query.shape[2:]
    words = text_kv.shape[1]
    bf16, f32 = jnp.bfloat16, jnp.float32
    heads = (GROUP, rows, HEAD)
    anywhere = pl.BlockSpec(memory_space=pl.ANY)
    scalars = pl.BlockSpec(memory_space=pltpu.SMEM)
    by_slot = pl.pallas_call(
        kernel,
        out_shape=jax.ShapeDtypeStruct((HEADS, rows, HEAD), bf16),
        in_specs=[anywhere] * 5 + [scalars] * 2,
        out_specs=anywhere,
        scratch_shapes=[
            pltpu.VMEM((HEADS, rows, HEAD), bf16),
            pltpu.VMEM((HEADS, rows, HEAD), bf16),
            pltpu.VMEM((HEADS, rows, HEAD), bf16),
            pltpu.VMEM((HEADS, 2, rows, HEAD), bf16),
            pltpu.VMEM((2, 4, 2, HEADS, 2, words, HEAD), bf16),
            pltpu.VMEM((2, *heads), bf16),
            pltpu.VMEM((2, *heads), bf16),
            pltpu.VMEM((2, *heads), bf16),
            pltpu.VMEM(heads, bf16),
            pltpu.VMEM((2, 2, *heads), bf16),
            pltpu.VMEM((2, 2, *heads), bf16),
            pltpu.VMEM((2, 2, *heads), bf16),
            pltpu.VMEM((2, *heads), bf16),
            pltpu.VMEM((2, *heads), bf16),
            pltpu.VMEM((2, 8, rows), f32),
            pltpu.VMEM((2, *heads), bf16),
            pltpu.VMEM((2, 8, rows), f32),
            [pltpu.VMEM((5, rows, LANES), f32)] * GROUP,
            [pltpu.VMEM((5, rows, LANES), f32)] * GROUP,
            [pltpu.VMEM((5, rows, HEAD), f32)] * GROUP,
            pltpu.VMEM((HEADS, rows, HEAD), bf16),
            pltpu.SMEM((HEADS,), jnp.int32),
            pltpu.VMEM((2, *heads), bf16),
            pltpu.SemaphoreType.DMA((5,)),
            pltpu.SemaphoreType.DMA((6, 2)),
            pltpu.SemaphoreType.DMA((6, 2)),
            pltpu.SemaphoreType.DMA((5,)),
            pltpu.SemaphoreType.DMA((5,)),
            pltpu.SemaphoreType.DMA(()),
            pltpu.SemaphoreType.DMA((2 * GROUP,)),
            pltpu.SemaphoreType.DMA((4,)),
        ],
        compiler_params=pltpu.CompilerParams(
            collective_id=0, has_side_effects=True, vmem_limit_bytes=60 << 20
        ),
    )(
        query[0, 0], fresh_key[0, 0], fresh_value[0, 0], stale_kv[:, 0, 0], text_kv,
        window.T, text_len,
    )
    result = pl.pallas_call(
        arrange,
        out_shape=jax.ShapeDtypeStruct((rows, width), bf16),
        in_specs=[anywhere, scalars],
        out_specs=anywhere,
        scratch_shapes=[
            pltpu.VMEM((HEADS, rows, HEAD), bf16),
            pltpu.SemaphoreType.DMA((HEADS,)),
            pltpu.SemaphoreType.DMA((HEADS,)),
        ],
        compiler_params=pltpu.CompilerParams(vmem_limit_bytes=60 << 20),
    )(by_slot, window.T)
    return result[None, None]


def solution(mesh):
    in_specs = (
        P("tm", "space", None, None),
        P("tm", "space", None, None),
        P("tm", "space", None, None),
        P(None, "tm", "space", None, None),
        P(None, "space", None),
        P(),
        P(),
    )
    out_specs = P("tm", "space", None, None)
    return jax.shard_map(
        on_device, mesh=mesh, in_specs=in_specs, out_specs=out_specs, check_vma=False
    )
```

```python
import functools
import math

import jax
import jax.numpy as jnp
from jax import lax
from jax.experimental import pallas as pl
from jax.experimental.pallas import tpu as pltpu
from jax.sharding import PartitionSpec as P

MESH = pl.DeviceIdType.MESH
HEAD = 128
GROUP = 3
HEADS = 12
LANES = 128
ROW_BLOCK = 384


def slots_of(window):
    counts = [jnp.int32(0)] * 4
    slots = []
    for head in range(HEADS):
        reach_time, reach_space = window[0, head], window[1, head]
        both = reach_time * reach_space
        hits = [both, reach_time - both, reach_space - both, 1 - reach_time - reach_space + both]
        slot = jnp.int32(0)
        for k in range(4):
            slot = slot + hits[k] * (GROUP * k + counts[k])
            counts[k] = counts[k] + hits[k]
        slots.append(slot)
    return slots


def kernel(
    query, fresh_key, fresh_value, stale, text, window, text_len, out,
    q_all, k_all, v_all, stale_all, words, out_all,
    pack11, sides, packq,
    got11, got_sides, gotq,
    o_send, o_stat, o_got, o_got_stat,
    peak, total, mixed, done, order, place,
    relay, load_sem, send_sem, recv_sem, text_send, text_recv, relay_send, relay_recv,
):
    rows = q_all.shape[1]
    pack10, pack01 = sides.at[0], sides.at[1]
    got10, got01 = got_sides.at[0], got_sides.at[1]
    times = lax.axis_size("tm")
    spaces = lax.axis_size("space")
    time = lax.axis_index("tm")
    space = lax.axis_index("space")
    core = lax.rem(space, 2)
    low = lax.rem(space // 2, 2)
    column = space // 4
    has_time = (time > 0, time < times - 1)
    has_space = (space > 0, space < spaces - 1)
    next_time = (time - 1, time + 1)
    next_space = (space - 1, space + 1)
    middle = times // 2
    inner = jnp.logical_or(time == middle - 1, time == middle)
    straight = (
        jnp.logical_and(has_time[0], time != middle),
        jnp.logical_and(has_time[1], time != middle - 1),
    )
    bent = (time == middle, time == middle - 1)
    scale = math.log2(math.e) / math.sqrt(HEAD)

    mine = words.at[core, column, low]
    lanes = [pl.ds(head * HEAD, HEAD) for head in range(HEADS)]
    for head, at in enumerate(lanes):
        pltpu.make_async_copy(text.at[:, :, at], mine.at[head], load_sem.at[2]).start()
    for head, at in enumerate(lanes):
        pltpu.make_async_copy(stale.at[:, :, at], stale_all.at[head], load_sem.at[0]).start()
    for head, at in enumerate(lanes):
        pltpu.make_async_copy(query.at[:, at], q_all.at[head], load_sem.at[1]).start()
    loads = [
        pltpu.make_async_copy(target, target, load_sem.at[i])
        for i, target in enumerate((stale_all, q_all, mine, k_all, v_all))
    ]

    partner_low = column * 4 + (1 - low) * 2 + core
    sibling = space + 1 - 2 * core
    barrier = pltpu.get_barrier_semaphore()
    for d in (0, 1):
        @pl.when(has_time[d])
        def _():
            pl.semaphore_signal(barrier, inc=1, device_id={"tm": time - 1 + 2 * d}, device_id_type=MESH)

        @pl.when(has_space[d])
        def _():
            pl.semaphore_signal(barrier, inc=1, device_id={"space": space - 1 + 2 * d}, device_id_type=MESH)

    partners = [partner_low] + [lax.rem(space + 4 * d, spaces) for d in (1, 2, 3)]
    for partner in partners:
        pl.semaphore_signal(barrier, inc=1, device_id={"space": partner}, device_id_type=MESH)

    @pl.when(inner)
    def _():
        opposite = {"tm": 2 * middle - 1 - time, "space": partner_low}
        pl.semaphore_signal(barrier, inc=1, device_id=opposite, device_id_type=MESH)

    greeted = len(partners) + sum(has.astype(jnp.int32) for has in has_time + has_space)
    greeted = greeted + inner.astype(jnp.int32)

    slots = slots_of(window)
    for head in range(HEADS):
        place[head] = jnp.minimum(slots[head], HEADS - 1)
    for s in range(HEADS):
        chosen = jnp.int32(0)
        for head in range(HEADS):
            apart = jnp.maximum(slots[head] - s, s - slots[head])
            chosen = chosen + head * jnp.maximum(1 - apart, 0)
        order[s] = chosen

    def pack(target, base):
        for g in range(GROUP):
            target[:, g] = stale_all[order[base + g]]

    def along_time(kind, d, source, target):
        return pltpu.make_async_remote_copy(
            src_ref=source, dst_ref=target.at[1 - d],
            send_sem=send_sem.at[kind, d], recv_sem=recv_sem.at[kind, 1 - d],
            device_id={"tm": time - 1 + 2 * d}, device_id_type=MESH,
        )

    def along_space(kind, d, source, target):
        return pltpu.make_async_remote_copy(
            src_ref=source, dst_ref=target.at[1 - d],
            send_sem=send_sem.at[kind, d], recv_sem=recv_sem.at[kind, 1 - d],
            device_id={"space": space - 1 + 2 * d}, device_id_type=MESH,
        )

    def send_both(has, make, kind, source, target):
        for d in (0, 1):
            @pl.when(has[d])
            def _():
                make(kind, d, source, target).start()

    def arrived(has, make, kind, source, target):
        for d in (0, 1):
            @pl.when(has[d])
            def _():
                make(kind, 1 - d, source, target).wait_recv()

    def sent(has, make, kind, source, target):
        for d in (0, 1):
            @pl.when(has[d])
            def _():
                make(kind, d, source, target).wait_send()

    spread = [
        pltpu.make_async_remote_copy(
            src_ref=words.at[core, column], dst_ref=words.at[core, column],
            send_sem=text_send.at[d], recv_sem=text_recv.at[d],
            device_id={"space": lax.rem(space + 4 * d, spaces)}, device_id_type=MESH,
        )
        for d in (1, 2, 3)
    ]
    swap = pltpu.make_async_remote_copy(
        src_ref=mine, dst_ref=mine, send_sem=text_send.at[0], recv_sem=text_recv.at[0],
        device_id={"space": partner_low}, device_id_type=MESH,
    )
    loads[2].wait()
    pl.semaphore_wait(barrier, greeted)
    swap.start()
    loads[0].wait()
    pack(pack11, 0)
    send_both(has_time, along_time, 0, pack11, got11)
    for head, at in enumerate(lanes):
        pltpu.make_async_copy(fresh_key.at[:, at], k_all.at[head], load_sem.at[3]).start()
        pltpu.make_async_copy(fresh_value.at[:, at], v_all.at[head], load_sem.at[4]).start()
    swap.wait_recv()
    for copy in spread:
        copy.start()
    loads[1].wait()
    for g in range(GROUP):
        packq[g] = q_all[order[g]]
    send_both(has_space, along_space, 3, packq, gotq)
    pack(pack10, GROUP)

    pieces = [(kv, g) for g in range(GROUP) for kv in range(2)]

    def detour(d, i):
        kv, g = pieces[i]
        return pltpu.make_async_remote_copy(
            src_ref=pack10.at[kv, g], dst_ref=relay.at[kv, g],
            send_sem=send_sem.at[1, d], recv_sem=relay_recv.at[i],
            device_id={"space": partner_low}, device_id_type=MESH,
        )

    def onward(d, i):
        kv, g = pieces[i]
        return pltpu.make_async_remote_copy(
            src_ref=relay.at[kv, g], dst_ref=got10.at[1 - d, kv, g],
            send_sem=relay_send, recv_sem=recv_sem.at[1, 1 - d],
            device_id={"tm": time - 1 + 2 * d, "space": partner_low}, device_id_type=MESH,
        )

    for d in (0, 1):
        @pl.when(bent[d])
        def _():
            for i in range(len(pieces)):
                detour(d, i).start()

    pack(pack01, 2 * GROUP)
    send_both(has_space, along_space, 2, pack01, got01)

    def rows_at(block):
        return pl.ds(block * ROW_BLOCK, ROW_BLOCK)

    def attend(jobs):
        for job in jobs:
            job["keys"] = jnp.concatenate([chunk[0] for chunk in job["chunks"]], axis=0)
            values = jnp.concatenate([chunk[1] for chunk in job["chunks"]], axis=0)
            ones = jnp.ones((values.shape[0], LANES), jnp.bfloat16)
            job["values"] = jnp.concatenate([values, ones], axis=1)
        tasks = [dict(job, here=rows_at(block)) for job in jobs for block in range(rows // ROW_BLOCK)]

        def score(task):
            query_rows = task["query"](task["here"])
            task["scores"] = lax.dot_general(
                query_rows, task["keys"], (((1,), (1,)), ((), ())),
                preferred_element_type=jnp.float32,
            ) * scale

        def weigh(task):
            pieces, tops, at = [], [], 0
            before = task["before"](task["here"]) if task["before"] else None
            for keys, _, live, valid in task["chunks"]:
                piece = task["scores"][:, at : at + keys.shape[0]]
                at += keys.shape[0]
                if live is not None:
                    piece = jnp.where(live, piece, -1e30)
                top = jnp.broadcast_to(jnp.max(piece, axis=1, keepdims=True), (ROW_BLOCK, LANES))
                if valid is not None:
                    top = jnp.where(valid, top, -1e30)
                pieces.append(piece)
                tops.append(top)
            top = functools.reduce(jnp.maximum, tops + ([before[0]] if before else []))
            weights = []
            for piece, (_, _, _, valid) in zip(pieces, task["chunks"]):
                base = top if valid is None else jnp.where(valid, top, 1e30)
                base = jnp.concatenate([base] * (piece.shape[1] // LANES), axis=1)
                weights.append(jnp.exp2(piece - base).astype(jnp.bfloat16))
            both = jnp.dot(
                jnp.concatenate(weights, axis=1), task["values"], preferred_element_type=jnp.float32
            )
            mixed, total = both[:, :HEAD], both[:, HEAD:]
            if before:
                shrink = jnp.exp2(before[0] - top)
                total = before[1] * shrink + total
                mixed = before[2] * shrink + mixed
            task["after"](task["here"], top, total, mixed)

        score(tasks[0])
        for i, task in enumerate(tasks):
            if i + 1 < len(tasks):
                score(tasks[i + 1])
            weigh(task)

    def job(query, chunks, after, before=None):
        return {"query": query, "chunks": chunks, "before": before, "after": after}

    def own(slot):
        head = order[slot]
        return lambda here: q_all[head, here]

    def saved(g, state):
        return lambda here: (peak[g][state, here], total[g][state, here], mixed[g][state, here])

    def save(g, state):
        def after(here, top, weight, value):
            peak[g][state, here] = top
            total[g][state, here] = weight
            mixed[g][state, here] = value

        return after

    def finish(target, at):
        def after(here, top, weight, value):
            target[(*at, here)] = (value / weight).astype(jnp.bfloat16)

        return after

    def fresh(slot):
        head = order[slot]
        return k_all[head], v_all[head], None, None

    def spoken(slot):
        head = order[slot]
        keys = words[:, :, :, head, 0].reshape(count, HEAD)
        values = words[:, :, :, head, 1].reshape(count, HEAD)
        return keys, values, live, None

    def near(got, g, has):
        return [(got[e, 0, g], got[e, 1, g], None, has[e]) for e in (0, 1)]

    def side_ok(d, position, count):
        return jnp.where(d == 0, position > 0, position < count - 1)

    count = 2 * spaces // 2 * words.shape[5]
    index = lax.broadcasted_iota(jnp.int32, (1, count), 1)
    token = (((index // 32) % 4) * 4 + ((index // 16) % 2) * 2 + index // 128) * 16 + index % 16
    live = token < text_len[0]

    for d in (0, 1):
        @pl.when(jnp.logical_not(has_time[d]))
        def _():
            got11[d] = jnp.zeros_like(got11[d])
            got10[d] = jnp.zeros_like(got10[d])

        @pl.when(jnp.logical_not(has_space[d]))
        def _():
            got01[d] = jnp.zeros_like(got01[d])
            o_got[d] = jnp.zeros_like(o_got[d])
            o_got_stat[d] = jnp.full_like(o_got_stat[d], -1e30)

    loads[3].wait()
    loads[4].wait()

    @pl.loop(0, 3)
    def _(kind):
        attend([
            job(own(kind * GROUP + g), [fresh(kind * GROUP + g)], save(g, kind))
            for g in range(GROUP)
        ])

    arrived(has_space, along_space, 3, packq, gotq)

    def visitor(d, g):
        return lambda here: gotq[d, g, here]

    @pl.loop(0, 2)
    def _(d):
        @pl.when(side_ok(d, space, spaces))
        def _():
            attend([
                job(visitor(d, g), [(pack11[0, g], pack11[1, g], None, None)], save(g, 3 + d))
                for g in range(GROUP)
            ])

    for d in (0, 1):
        @pl.when(straight[d])
        def _():
            along_time(0, d, pack11, got11).wait_send()
            along_time(1, d, pack10, got10).start()

    for copy in spread:
        copy.wait_recv()
    half = words.at[core]
    across = pltpu.make_async_remote_copy(
        src_ref=half, dst_ref=half, send_sem=text_send.at[4], recv_sem=text_recv.at[4],
        device_id={"space": sibling}, device_id_type=MESH,
    )
    across.start()

    for d in (0, 1):
        @pl.when(bent[d])
        def _():
            for i in range(len(pieces)):
                detour(d, i).wait_recv()
                onward(d, i).start()

    arrived(has_time, along_time, 0, pack11, got11)
    lane = lax.broadcasted_iota(jnp.int32, (rows, LANES), 1)

    @pl.loop(0, 2)
    def _(i):
        d = lax.rem(i + core, 2)

        @pl.when(side_ok(d, space, spaces))
        def _():
            def give(g):
                def after(here, top, weight, value):
                    o_send[d, g, here] = (value / weight).astype(jnp.bfloat16)
                    peak[g][3 + d, here] = top + jnp.log2(weight)

                return after

            attend([
                job(visitor(d, g), near(got11, g, has_time), give(g), saved(g, 3 + d))
                for g in range(GROUP)
            ])
            stats = jnp.zeros((rows, LANES), jnp.float32)
            for g in range(GROUP):
                stats = jnp.where(lane == g, peak[g][3 + d], stats)
            o_stat[d] = stats.T[:8]
            along_space(4, d, o_send.at[d], o_got).start()
            along_space(5, d, o_stat.at[d], o_got_stat).start()

    across.wait_recv()
    attend([
        job(own(3 * GROUP + g), [fresh(3 * GROUP + g), spoken(3 * GROUP + g)], finish(done, (3 * GROUP + g,)))
        for g in range(GROUP)
    ])

    attend([
        job(own(g), [spoken(g), *near(got11, g, has_time)], save(g, 0), saved(g, 0))
        for g in range(GROUP)
    ])
    outer = jnp.logical_or(time == 0, time == times - 1)

    @pl.loop(0, 2)
    def _(i):
        k = jnp.where(outer, i, 1 - i)

        @pl.when(k == 0)
        def _():
            arrived(has_time, along_time, 1, pack10, got10)

        @pl.when(k == 1)
        def _():
            arrived(has_space, along_space, 2, pack01, got01)

        valid = [jnp.where(k == 0, has_time[e], has_space[e]) for e in (0, 1)]
        attend([
            job(
                own((1 + k) * GROUP + g),
                [spoken((1 + k) * GROUP + g)]
                + [(got_sides[k, e, 0, g], got_sides[k, e, 1, g], None, valid[e]) for e in (0, 1)],
                finish(done, ((1 + k) * GROUP + g,)),
                saved(g, 1 + k),
            )
            for g in range(GROUP)
        ])

    logs = []
    for d in (0, 1):
        @pl.when(has_space[d])
        def _():
            along_space(4, 1 - d, o_send.at[1 - d], o_got).wait_recv()
            along_space(5, 1 - d, o_stat.at[1 - d], o_got_stat).wait_recv()

        spare = jnp.zeros((LANES - 8, rows), jnp.float32)
        logs.append(jnp.concatenate([o_got_stat[d], spare], axis=0).T)
    for g in range(GROUP):
        others = [jnp.broadcast_to(log[:, g : g + 1], (rows, LANES)) for log in logs]
        top = jnp.maximum(peak[g][0], jnp.maximum(*others))
        keep = jnp.exp2(peak[g][0] - top)
        add = [jnp.exp2(other - top) for other in others]
        value = mixed[g][0] * keep
        for d in (0, 1):
            value = value + o_got[d, g].astype(jnp.float32) * add[d]
        done[g] = (value / (total[g][0] * keep + add[0] + add[1])).astype(jnp.bfloat16)

    for head in range(HEADS):
        out_all[:, head * HEAD : (head + 1) * HEAD] = done[place[head]]
    store = pltpu.make_async_copy(out_all, out, load_sem.at[5])
    store.start()

    for d in (0, 1):
        @pl.when(bent[d])
        def _():
            along_time(0, d, pack11, got11).wait_send()

    sent(has_time, along_time, 1, pack10, got10)

    @pl.when(inner)
    def _():
        pltpu.make_async_copy(relay, relay, relay_send).wait()

    sent(has_space, along_space, 2, pack01, got01)
    sent(has_space, along_space, 3, packq, gotq)
    for d in (0, 1):
        @pl.when(has_space[d])
        def _():
            along_space(4, d, o_send.at[d], o_got).wait_send()
            along_space(5, d, o_stat.at[d], o_got_stat).wait_send()
    swap.wait_send()
    for copy in spread:
        copy.wait_send()
    across.wait_send()
    store.wait()


def on_device(query, fresh_key, fresh_value, stale_kv, text_kv, window, text_len):
    rows, width = query.shape[2:]
    words = text_kv.shape[1]
    bf16, f32 = jnp.bfloat16, jnp.float32
    heads = (GROUP, rows, HEAD)
    scalars = pl.BlockSpec(memory_space=pltpu.SMEM)
    result = pl.pallas_call(
        kernel,
        out_shape=jax.ShapeDtypeStruct((rows, width), bf16),
        in_specs=[pl.BlockSpec(memory_space=pltpu.HBM)] * 5 + [scalars] * 2,
        out_specs=pl.BlockSpec(memory_space=pl.ANY),
        scratch_shapes=[
            pltpu.VMEM((HEADS, rows, HEAD), bf16),
            pltpu.VMEM((HEADS, rows, HEAD), bf16),
            pltpu.VMEM((HEADS, rows, HEAD), bf16),
            pltpu.VMEM((HEADS, 2, rows, HEAD), bf16),
            pltpu.VMEM((2, 4, 2, HEADS, 2, words, HEAD), bf16),
            pltpu.VMEM((rows, width), bf16),
            pltpu.VMEM((2, *heads), bf16),
            pltpu.VMEM((2, 2, *heads), bf16),
            pltpu.VMEM(heads, bf16),
            pltpu.VMEM((2, 2, *heads), bf16),
            pltpu.VMEM((2, 2, 2, *heads), bf16),
            pltpu.VMEM((2, *heads), bf16),
            pltpu.VMEM((2, *heads), bf16),
            pltpu.VMEM((2, 8, rows), f32),
            pltpu.VMEM((2, *heads), bf16),
            pltpu.VMEM((2, 8, rows), f32),
            [pltpu.VMEM((5, rows, LANES), f32)] * GROUP,
            [pltpu.VMEM((5, rows, LANES), f32)] * GROUP,
            [pltpu.VMEM((5, rows, HEAD), f32)] * GROUP,
            pltpu.VMEM((HEADS, rows, HEAD), bf16),
            pltpu.SMEM((HEADS,), jnp.int32),
            pltpu.SMEM((HEADS,), jnp.int32),
            pltpu.VMEM((2, *heads), bf16),
            pltpu.SemaphoreType.DMA((6,)),
            pltpu.SemaphoreType.DMA((6, 2)),
            pltpu.SemaphoreType.DMA((6, 2)),
            pltpu.SemaphoreType.DMA((5,)),
            pltpu.SemaphoreType.DMA((5,)),
            pltpu.SemaphoreType.DMA(()),
            pltpu.SemaphoreType.DMA((2 * GROUP,)),
        ],
        compiler_params=pltpu.CompilerParams(
            collective_id=0, has_side_effects=True, vmem_limit_bytes=52 << 20
        ),
    )(
        query[0, 0], fresh_key[0, 0], fresh_value[0, 0], stale_kv[:, 0, 0], text_kv,
        window.T, text_len,
    )
    return result[None, None]


def solution(mesh):
    in_specs = (
        P("tm", "space", None, None),
        P("tm", "space", None, None),
        P("tm", "space", None, None),
        P(None, "tm", "space", None, None),
        P(None, "space", None),
        P(),
        P(),
    )
    out_specs = P("tm", "space", None, None)
    return jax.shard_map(
        on_device, mesh=mesh, in_specs=in_specs, out_specs=out_specs, check_vma=False
    )
```

```python
import functools
import math

import jax
import jax.numpy as jnp
from jax import lax
from jax.experimental import pallas as pl
from jax.experimental.pallas import tpu as pltpu
from jax.sharding import PartitionSpec as P

MESH = pl.DeviceIdType.MESH
HEAD = 128
GROUP = 3
HEADS = 12
LANES = 128
ROW_BLOCK = 384


def slots_of(window):
    counts = [jnp.int32(0)] * 4
    slots = []
    for head in range(HEADS):
        reach_time, reach_space = window[0, head], window[1, head]
        both = reach_time * reach_space
        hits = [both, reach_time - both, reach_space - both, 1 - reach_time - reach_space + both]
        slot = jnp.int32(0)
        for k in range(4):
            slot = slot + hits[k] * (GROUP * k + counts[k])
            counts[k] = counts[k] + hits[k]
        slots.append(slot)
    return slots


def kernel(
    query, fresh_key, fresh_value, stale, text, window, text_len, out,
    q_all, k_all, v_all, stale_all, words, out_all,
    pack11, sides, packq,
    got11, got_sides, gotq,
    o_send, o_stat, o_got, o_got_stat,
    peak, total, mixed, done, order, place,
    relay, hosted, load_sem, send_sem, recv_sem, text_send, text_recv, relay_send, relay_recv, hosted_send, hosted_recv,
):
    rows = q_all.shape[1]
    pack10, pack01 = sides.at[0], sides.at[1]
    got10, got01 = got_sides.at[0], got_sides.at[1]
    times = lax.axis_size("tm")
    spaces = lax.axis_size("space")
    time = lax.axis_index("tm")
    space = lax.axis_index("space")
    core = lax.rem(space, 2)
    low = lax.rem(space // 2, 2)
    column = space // 4
    has_time = (time > 0, time < times - 1)
    has_space = (space > 0, space < spaces - 1)
    next_time = (time - 1, time + 1)
    next_space = (space - 1, space + 1)
    middle = times // 2
    inner = jnp.logical_or(time == middle - 1, time == middle)
    straight = (
        jnp.logical_and(has_time[0], time != middle),
        jnp.logical_and(has_time[1], time != middle - 1),
    )
    bent = (time == middle, time == middle - 1)
    loaded = jnp.logical_or(jnp.logical_or(time == 0, time == times - 1), inner)
    inward = jnp.where(jnp.logical_or(time == 0, time == middle), time + 1, time - 1)
    host = functools.reduce(
        jnp.logical_or, [time == 1, time == middle - 2, time == middle + 1, time == times - 2]
    )
    guest = jnp.where(jnp.logical_or(time == 1, time == middle + 1), time - 1, time + 1)
    crossing = (
        jnp.logical_and(has_space[0], lax.rem(space, 4) == 0),
        jnp.logical_and(has_space[1], lax.rem(space, 4) == 3),
    )
    hopping = [jnp.logical_and(loaded, crossing[d]) for d in (0, 1)]
    hosting = [jnp.logical_and(host, crossing[d]) for d in (0, 1)]
    direct = [jnp.logical_and(has_space[d], jnp.logical_not(hopping[d])) for d in (0, 1)]
    scale = math.log2(math.e) / math.sqrt(HEAD)

    mine = words.at[core, column, low]
    lanes = [pl.ds(head * HEAD, HEAD) for head in range(HEADS)]
    for head, at in enumerate(lanes):
        pltpu.make_async_copy(text.at[:, :, at], mine.at[head], load_sem.at[2]).start()
    for head, at in enumerate(lanes):
        pltpu.make_async_copy(stale.at[:, :, at], stale_all.at[head], load_sem.at[0]).start()
    for head, at in enumerate(lanes):
        pltpu.make_async_copy(query.at[:, at], q_all.at[head], load_sem.at[1]).start()
    loads = [
        pltpu.make_async_copy(target, target, load_sem.at[i])
        for i, target in enumerate((stale_all, q_all, mine, k_all, v_all))
    ]

    partner_low = column * 4 + (1 - low) * 2 + core
    sibling = space + 1 - 2 * core
    barrier = pltpu.get_barrier_semaphore()
    for d in (0, 1):
        @pl.when(has_time[d])
        def _():
            pl.semaphore_signal(barrier, inc=1, device_id={"tm": time - 1 + 2 * d}, device_id_type=MESH)

        @pl.when(has_space[d])
        def _():
            pl.semaphore_signal(barrier, inc=1, device_id={"space": space - 1 + 2 * d}, device_id_type=MESH)

    partners = [partner_low] + [lax.rem(space + 4 * d, spaces) for d in (1, 2, 3)]
    for partner in partners:
        pl.semaphore_signal(barrier, inc=1, device_id={"space": partner}, device_id_type=MESH)

    @pl.when(inner)
    def _():
        opposite = {"tm": 2 * middle - 1 - time, "space": partner_low}
        pl.semaphore_signal(barrier, inc=1, device_id=opposite, device_id_type=MESH)

    for d in (0, 1):
        @pl.when(hopping[d])
        def _():
            ahead = {"tm": inward, "space": space - 1 + 2 * d}
            pl.semaphore_signal(barrier, inc=1, device_id=ahead, device_id_type=MESH)

        @pl.when(hosting[d])
        def _():
            behind = {"tm": guest, "space": space - 1 + 2 * d}
            pl.semaphore_signal(barrier, inc=1, device_id=behind, device_id_type=MESH)

    greeted = len(partners) + sum(has.astype(jnp.int32) for has in has_time + has_space)
    greeted = greeted + inner.astype(jnp.int32)
    greeted = greeted + sum(hop.astype(jnp.int32) for hop in hopping + hosting)

    slots = slots_of(window)
    for head in range(HEADS):
        place[head] = jnp.minimum(slots[head], HEADS - 1)
    for s in range(HEADS):
        chosen = jnp.int32(0)
        for head in range(HEADS):
            apart = jnp.maximum(slots[head] - s, s - slots[head])
            chosen = chosen + head * jnp.maximum(1 - apart, 0)
        order[s] = chosen

    def pack(target, base):
        for g in range(GROUP):
            target[:, g] = stale_all[order[base + g]]

    def along_time(kind, d, source, target):
        return pltpu.make_async_remote_copy(
            src_ref=source, dst_ref=target.at[1 - d],
            send_sem=send_sem.at[kind, d], recv_sem=recv_sem.at[kind, 1 - d],
            device_id={"tm": time - 1 + 2 * d}, device_id_type=MESH,
        )

    def along_space(kind, d, source, target):
        return pltpu.make_async_remote_copy(
            src_ref=source, dst_ref=target.at[1 - d],
            send_sem=send_sem.at[kind, d], recv_sem=recv_sem.at[kind, 1 - d],
            device_id={"space": space - 1 + 2 * d}, device_id_type=MESH,
        )

    def send_both(has, make, kind, source, target):
        for d in (0, 1):
            @pl.when(has[d])
            def _():
                make(kind, d, source, target).start()

    def arrived(has, make, kind, source, target):
        for d in (0, 1):
            @pl.when(has[d])
            def _():
                make(kind, 1 - d, source, target).wait_recv()

    def sent(has, make, kind, source, target):
        for d in (0, 1):
            @pl.when(has[d])
            def _():
                make(kind, d, source, target).wait_send()

    spread = [
        pltpu.make_async_remote_copy(
            src_ref=words.at[core, column], dst_ref=words.at[core, column],
            send_sem=text_send.at[d], recv_sem=text_recv.at[d],
            device_id={"space": lax.rem(space + 4 * d, spaces)}, device_id_type=MESH,
        )
        for d in (1, 2, 3)
    ]
    swap = pltpu.make_async_remote_copy(
        src_ref=mine, dst_ref=mine, send_sem=text_send.at[0], recv_sem=text_recv.at[0],
        device_id={"space": partner_low}, device_id_type=MESH,
    )
    loads[2].wait()
    pl.semaphore_wait(barrier, greeted)
    swap.start()
    loads[0].wait()
    pack(pack11, 0)
    send_both(has_time, along_time, 0, pack11, got11)
    for head, at in enumerate(lanes):
        pltpu.make_async_copy(fresh_key.at[:, at], k_all.at[head], load_sem.at[3]).start()
        pltpu.make_async_copy(fresh_value.at[:, at], v_all.at[head], load_sem.at[4]).start()
    swap.wait_recv()
    for copy in spread:
        copy.start()
    loads[1].wait()
    for g in range(GROUP):
        packq[g] = q_all[order[g]]
    send_both(has_space, along_space, 3, packq, gotq)
    pack(pack10, GROUP)

    pieces = [(kv, g) for g in range(GROUP) for kv in range(2)]

    def detour(d, i):
        kv, g = pieces[i]
        return pltpu.make_async_remote_copy(
            src_ref=pack10.at[kv, g], dst_ref=relay.at[kv, g],
            send_sem=send_sem.at[1, d], recv_sem=relay_recv.at[i],
            device_id={"space": partner_low}, device_id_type=MESH,
        )

    def onward(d, i):
        kv, g = pieces[i]
        return pltpu.make_async_remote_copy(
            src_ref=relay.at[kv, g], dst_ref=got10.at[1 - d, kv, g],
            send_sem=relay_send, recv_sem=recv_sem.at[1, 1 - d],
            device_id={"tm": time - 1 + 2 * d, "space": partner_low}, device_id_type=MESH,
        )

    for d in (0, 1):
        @pl.when(bent[d])
        def _():
            for i in range(len(pieces)):
                detour(d, i).start()

    pack(pack01, 2 * GROUP)
    send_both(direct, along_space, 2, pack01, got01)

    def hop(d, i):
        kv, g = pieces[i]
        return pltpu.make_async_remote_copy(
            src_ref=pack01.at[kv, g], dst_ref=hosted.at[kv, g],
            send_sem=send_sem.at[2, d], recv_sem=hosted_recv.at[i],
            device_id={"tm": inward, "space": space - 1 + 2 * d}, device_id_type=MESH,
        )

    def home(d, i):
        kv, g = pieces[i]
        return pltpu.make_async_remote_copy(
            src_ref=hosted.at[kv, g], dst_ref=got01.at[d, kv, g],
            send_sem=hosted_send, recv_sem=recv_sem.at[2, d],
            device_id={"tm": guest}, device_id_type=MESH,
        )

    for d in (0, 1):
        @pl.when(hopping[d])
        def _():
            for i in range(len(pieces)):
                hop(d, i).start()

    def rows_at(block):
        return pl.ds(block * ROW_BLOCK, ROW_BLOCK)

    def attend(jobs):
        for job in jobs:
            job["keys"] = jnp.concatenate([chunk[0] for chunk in job["chunks"]], axis=0)
            values = jnp.concatenate([chunk[1] for chunk in job["chunks"]], axis=0)
            ones = jnp.ones((values.shape[0], LANES), jnp.bfloat16)
            job["values"] = jnp.concatenate([values, ones], axis=1)
        tasks = [dict(job, here=rows_at(block)) for job in jobs for block in range(rows // ROW_BLOCK)]

        def score(task):
            query_rows = task["query"](task["here"])
            task["scores"] = lax.dot_general(
                query_rows, task["keys"], (((1,), (1,)), ((), ())),
                preferred_element_type=jnp.float32,
            ) * scale

        def weigh(task):
            pieces, tops, at = [], [], 0
            before = task["before"](task["here"]) if task["before"] else None
            for keys, _, live, valid in task["chunks"]:
                piece = task["scores"][:, at : at + keys.shape[0]]
                at += keys.shape[0]
                if live is not None:
                    piece = jnp.where(live, piece, -1e30)
                top = jnp.broadcast_to(jnp.max(piece, axis=1, keepdims=True), (ROW_BLOCK, LANES))
                if valid is not None:
                    top = jnp.where(valid, top, -1e30)
                pieces.append(piece)
                tops.append(top)
            top = functools.reduce(jnp.maximum, tops + ([before[0]] if before else []))
            weights = []
            for piece, (_, _, _, valid) in zip(pieces, task["chunks"]):
                base = top if valid is None else jnp.where(valid, top, 1e30)
                base = jnp.concatenate([base] * (piece.shape[1] // LANES), axis=1)
                weights.append(jnp.exp2(piece - base).astype(jnp.bfloat16))
            both = jnp.dot(
                jnp.concatenate(weights, axis=1), task["values"], preferred_element_type=jnp.float32
            )
            mixed, total = both[:, :HEAD], both[:, HEAD:]
            if before:
                shrink = jnp.exp2(before[0] - top)
                total = before[1] * shrink + total
                mixed = before[2] * shrink + mixed
            task["after"](task["here"], top, total, mixed)

        score(tasks[0])
        for i, task in enumerate(tasks):
            if i + 1 < len(tasks):
                score(tasks[i + 1])
            weigh(task)

    def job(query, chunks, after, before=None):
        return {"query": query, "chunks": chunks, "before": before, "after": after}

    def own(slot):
        head = order[slot]
        return lambda here: q_all[head, here]

    def saved(g, state):
        return lambda here: (peak[g][state, here], total[g][state, here], mixed[g][state, here])

    def save(g, state):
        def after(here, top, weight, value):
            peak[g][state, here] = top
            total[g][state, here] = weight
            mixed[g][state, here] = value

        return after

    def finish(target, at):
        def after(here, top, weight, value):
            target[(*at, here)] = (value / weight).astype(jnp.bfloat16)

        return after

    def fresh(slot):
        head = order[slot]
        return k_all[head], v_all[head], None, None

    def spoken(slot):
        head = order[slot]
        keys = words[:, :, :, head, 0].reshape(count, HEAD)
        values = words[:, :, :, head, 1].reshape(count, HEAD)
        return keys, values, live, None

    def near(got, g, has):
        return [(got[e, 0, g], got[e, 1, g], None, has[e]) for e in (0, 1)]

    def side_ok(d, position, count):
        return jnp.where(d == 0, position > 0, position < count - 1)

    count = 2 * spaces // 2 * words.shape[5]
    index = lax.broadcasted_iota(jnp.int32, (1, count), 1)
    token = (((index // 32) % 4) * 4 + ((index // 16) % 2) * 2 + index // 128) * 16 + index % 16
    live = token < text_len[0]

    for d in (0, 1):
        @pl.when(jnp.logical_not(has_time[d]))
        def _():
            got11[d] = jnp.zeros_like(got11[d])
            got10[d] = jnp.zeros_like(got10[d])

        @pl.when(jnp.logical_not(has_space[d]))
        def _():
            got01[d] = jnp.zeros_like(got01[d])
            o_got[d] = jnp.zeros_like(o_got[d])
            o_got_stat[d] = jnp.full_like(o_got_stat[d], -1e30)

    loads[3].wait()
    loads[4].wait()

    @pl.loop(0, 3)
    def _(kind):
        attend([
            job(own(kind * GROUP + g), [fresh(kind * GROUP + g)], save(g, kind))
            for g in range(GROUP)
        ])

    arrived(has_space, along_space, 3, packq, gotq)

    def visitor(d, g):
        return lambda here: gotq[d, g, here]

    @pl.loop(0, 2)
    def _(d):
        @pl.when(side_ok(d, space, spaces))
        def _():
            attend([
                job(visitor(d, g), [(pack11[0, g], pack11[1, g], None, None)], save(g, 3 + d))
                for g in range(GROUP)
            ])

    for d in (0, 1):
        @pl.when(straight[d])
        def _():
            along_time(0, d, pack11, got11).wait_send()
            along_time(1, d, pack10, got10).start()

    for copy in spread:
        copy.wait_recv()
    half = words.at[core]
    across = pltpu.make_async_remote_copy(
        src_ref=half, dst_ref=half, send_sem=text_send.at[4], recv_sem=text_recv.at[4],
        device_id={"space": sibling}, device_id_type=MESH,
    )
    across.start()

    for d in (0, 1):
        @pl.when(bent[d])
        def _():
            for i in range(len(pieces)):
                detour(d, i).wait_recv()
                onward(d, i).start()

    arrived(has_time, along_time, 0, pack11, got11)
    lane = lax.broadcasted_iota(jnp.int32, (rows, LANES), 1)

    @pl.loop(0, 2)
    def _(i):
        d = lax.rem(i + core, 2)

        @pl.when(side_ok(d, space, spaces))
        def _():
            def give(g):
                def after(here, top, weight, value):
                    o_send[d, g, here] = (value / weight).astype(jnp.bfloat16)
                    peak[g][3 + d, here] = top + jnp.log2(weight)

                return after

            attend([
                job(visitor(d, g), near(got11, g, has_time), give(g), saved(g, 3 + d))
                for g in range(GROUP)
            ])
            stats = jnp.zeros((rows, LANES), jnp.float32)
            for g in range(GROUP):
                stats = jnp.where(lane == g, peak[g][3 + d], stats)
            o_stat[d] = stats.T[:8]
            along_space(4, d, o_send.at[d], o_got).start()
            along_space(5, d, o_stat.at[d], o_got_stat).start()

    for d in (0, 1):
        @pl.when(hosting[d])
        def _():
            for i in range(len(pieces)):
                hop(d, i).wait_recv()
                home(d, i).start()

    across.wait_recv()
    attend([
        job(own(3 * GROUP + g), [fresh(3 * GROUP + g), spoken(3 * GROUP + g)], finish(done, (3 * GROUP + g,)))
        for g in range(GROUP)
    ])

    attend([
        job(own(g), [spoken(g), *near(got11, g, has_time)], save(g, 0), saved(g, 0))
        for g in range(GROUP)
    ])
    outer = jnp.logical_or(time == 0, time == times - 1)

    @pl.loop(0, 2)
    def _(i):
        k = jnp.where(outer, i, 1 - i)

        @pl.when(k == 0)
        def _():
            arrived(has_time, along_time, 1, pack10, got10)

        @pl.when(k == 1)
        def _():
            arrived(has_space, along_space, 2, pack01, got01)

        valid = [jnp.where(k == 0, has_time[e], has_space[e]) for e in (0, 1)]
        attend([
            job(
                own((1 + k) * GROUP + g),
                [spoken((1 + k) * GROUP + g)]
                + [(got_sides[k, e, 0, g], got_sides[k, e, 1, g], None, valid[e]) for e in (0, 1)],
                finish(done, ((1 + k) * GROUP + g,)),
                saved(g, 1 + k),
            )
            for g in range(GROUP)
        ])

    logs = []
    for d in (0, 1):
        @pl.when(has_space[d])
        def _():
            along_space(4, 1 - d, o_send.at[1 - d], o_got).wait_recv()
            along_space(5, 1 - d, o_stat.at[1 - d], o_got_stat).wait_recv()

        spare = jnp.zeros((LANES - 8, rows), jnp.float32)
        logs.append(jnp.concatenate([o_got_stat[d], spare], axis=0).T)
    for g in range(GROUP):
        others = [jnp.broadcast_to(log[:, g : g + 1], (rows, LANES)) for log in logs]
        top = jnp.maximum(peak[g][0], jnp.maximum(*others))
        keep = jnp.exp2(peak[g][0] - top)
        add = [jnp.exp2(other - top) for other in others]
        value = mixed[g][0] * keep
        for d in (0, 1):
            value = value + o_got[d, g].astype(jnp.float32) * add[d]
        done[g] = (value / (total[g][0] * keep + add[0] + add[1])).astype(jnp.bfloat16)

    for head in range(HEADS):
        out_all[:, head * HEAD : (head + 1) * HEAD] = done[place[head]]
    store = pltpu.make_async_copy(out_all, out, load_sem.at[5])
    store.start()

    for d in (0, 1):
        @pl.when(bent[d])
        def _():
            along_time(0, d, pack11, got11).wait_send()

    sent(has_time, along_time, 1, pack10, got10)

    @pl.when(inner)
    def _():
        pltpu.make_async_copy(relay, relay, relay_send).wait()

    @pl.when(jnp.logical_or(*hosting))
    def _():
        pltpu.make_async_copy(hosted, hosted, hosted_send).wait()

    sent(has_space, along_space, 2, pack01, got01)
    sent(has_space, along_space, 3, packq, gotq)
    for d in (0, 1):
        @pl.when(has_space[d])
        def _():
            along_space(4, d, o_send.at[d], o_got).wait_send()
            along_space(5, d, o_stat.at[d], o_got_stat).wait_send()
    swap.wait_send()
    for copy in spread:
        copy.wait_send()
    across.wait_send()
    store.wait()


def on_device(query, fresh_key, fresh_value, stale_kv, text_kv, window, text_len):
    rows, width = query.shape[2:]
    words = text_kv.shape[1]
    bf16, f32 = jnp.bfloat16, jnp.float32
    heads = (GROUP, rows, HEAD)
    scalars = pl.BlockSpec(memory_space=pltpu.SMEM)
    result = pl.pallas_call(
        kernel,
        out_shape=jax.ShapeDtypeStruct((rows, width), bf16),
        in_specs=[pl.BlockSpec(memory_space=pltpu.HBM)] * 5 + [scalars] * 2,
        out_specs=pl.BlockSpec(memory_space=pl.ANY),
        scratch_shapes=[
            pltpu.VMEM((HEADS, rows, HEAD), bf16),
            pltpu.VMEM((HEADS, rows, HEAD), bf16),
            pltpu.VMEM((HEADS, rows, HEAD), bf16),
            pltpu.VMEM((HEADS, 2, rows, HEAD), bf16),
            pltpu.VMEM((2, 4, 2, HEADS, 2, words, HEAD), bf16),
            pltpu.VMEM((rows, width), bf16),
            pltpu.VMEM((2, *heads), bf16),
            pltpu.VMEM((2, 2, *heads), bf16),
            pltpu.VMEM(heads, bf16),
            pltpu.VMEM((2, 2, *heads), bf16),
            pltpu.VMEM((2, 2, 2, *heads), bf16),
            pltpu.VMEM((2, *heads), bf16),
            pltpu.VMEM((2, *heads), bf16),
            pltpu.VMEM((2, 8, rows), f32),
            pltpu.VMEM((2, *heads), bf16),
            pltpu.VMEM((2, 8, rows), f32),
            [pltpu.VMEM((5, rows, LANES), f32)] * GROUP,
            [pltpu.VMEM((5, rows, LANES), f32)] * GROUP,
            [pltpu.VMEM((5, rows, HEAD), f32)] * GROUP,
            pltpu.VMEM((HEADS, rows, HEAD), bf16),
            pltpu.SMEM((HEADS,), jnp.int32),
            pltpu.SMEM((HEADS,), jnp.int32),
            pltpu.VMEM((2, *heads), bf16),
            pltpu.VMEM((2, *heads), bf16),
            pltpu.SemaphoreType.DMA((6,)),
            pltpu.SemaphoreType.DMA((6, 2)),
            pltpu.SemaphoreType.DMA((6, 2)),
            pltpu.SemaphoreType.DMA((5,)),
            pltpu.SemaphoreType.DMA((5,)),
            pltpu.SemaphoreType.DMA(()),
            pltpu.SemaphoreType.DMA((2 * GROUP,)),
            pltpu.SemaphoreType.DMA(()),
            pltpu.SemaphoreType.DMA((2 * GROUP,)),
        ],
        compiler_params=pltpu.CompilerParams(
            collective_id=0, has_side_effects=True, vmem_limit_bytes=52 << 20
        ),
    )(
        query[0, 0], fresh_key[0, 0], fresh_value[0, 0], stale_kv[:, 0, 0], text_kv,
        window.T, text_len,
    )
    return result[None, None]


def solution(mesh):
    in_specs = (
        P("tm", "space", None, None),
        P("tm", "space", None, None),
        P("tm", "space", None, None),
        P(None, "tm", "space", None, None),
        P(None, "space", None),
        P(),
        P(),
    )
    out_specs = P("tm", "space", None, None)
    return jax.shard_map(
        on_device, mesh=mesh, in_specs=in_specs, out_specs=out_specs, check_vma=False
    )
```

```python
import functools
import math

import jax
import jax.numpy as jnp
from jax import lax
from jax.experimental import pallas as pl
from jax.experimental.pallas import tpu as pltpu
from jax.sharding import PartitionSpec as P

MESH = pl.DeviceIdType.MESH
HEAD = 128
GROUP = 3
HEADS = 12
LANES = 128
ROW_BLOCK = 384


def slots_of(window):
    counts = [jnp.int32(0)] * 4
    slots = []
    for head in range(HEADS):
        reach_time, reach_space = window[0, head], window[1, head]
        both = reach_time * reach_space
        hits = [both, reach_time - both, reach_space - both, 1 - reach_time - reach_space + both]
        slot = jnp.int32(0)
        for k in range(4):
            slot = slot + hits[k] * (GROUP * k + counts[k])
            counts[k] = counts[k] + hits[k]
        slots.append(slot)
    return slots


def kernel(
    query, fresh_key, fresh_value, stale, text, window, text_len, out,
    q_all, k_all, v_all, stale_all, words, out_all,
    pack11, sides, packq,
    got11, got_sides, gotq,
    o_send, o_stat, o_got, o_got_stat,
    peak, total, mixed, done, order, place,
    relay, hosted, load_sem, send_sem, recv_sem, text_send, text_recv, relay_send, relay_recv, hosted_send, hosted_recv,
):
    rows = q_all.shape[1]
    pack10, pack01 = sides.at[0], sides.at[1]
    got10, got01 = got_sides.at[0], got_sides.at[1]
    times = lax.axis_size("tm")
    spaces = lax.axis_size("space")
    time = lax.axis_index("tm")
    space = lax.axis_index("space")
    core = lax.rem(space, 2)
    low = lax.rem(space // 2, 2)
    column = space // 4
    has_time = (time > 0, time < times - 1)
    has_space = (space > 0, space < spaces - 1)
    next_time = (time - 1, time + 1)
    next_space = (space - 1, space + 1)
    middle = times // 2
    inner = jnp.logical_or(time == middle - 1, time == middle)
    straight = (
        jnp.logical_and(has_time[0], time != middle),
        jnp.logical_and(has_time[1], time != middle - 1),
    )
    bent = (time == middle, time == middle - 1)
    loaded = jnp.logical_or(jnp.logical_or(time == 0, time == times - 1), inner)
    inward = jnp.where(jnp.logical_or(time == 0, time == middle), time + 1, time - 1)
    host = functools.reduce(
        jnp.logical_or, [time == 1, time == middle - 2, time == middle + 1, time == times - 2]
    )
    guest = jnp.where(jnp.logical_or(time == 1, time == middle + 1), time - 1, time + 1)
    crossing = (
        jnp.logical_and(has_space[0], lax.rem(space, 4) == 0),
        jnp.logical_and(has_space[1], lax.rem(space, 4) == 3),
    )
    hopping = [jnp.logical_and(loaded, crossing[d]) for d in (0, 1)]
    hosting = [jnp.logical_and(host, crossing[d]) for d in (0, 1)]
    direct = [jnp.logical_and(has_space[d], jnp.logical_not(hopping[d])) for d in (0, 1)]
    scale = math.log2(math.e) / math.sqrt(HEAD)

    partner_low = column * 4 + (1 - low) * 2 + core
    sibling = space + 1 - 2 * core
    barrier = pltpu.get_barrier_semaphore()
    for d in (0, 1):
        @pl.when(has_time[d])
        def _():
            pl.semaphore_signal(barrier, inc=1, device_id={"tm": time - 1 + 2 * d}, device_id_type=MESH)

        @pl.when(has_space[d])
        def _():
            pl.semaphore_signal(barrier, inc=1, device_id={"space": space - 1 + 2 * d}, device_id_type=MESH)

    partners = [partner_low] + [lax.rem(space + 4 * d, spaces) for d in (1, 2, 3)]
    for partner in partners:
        pl.semaphore_signal(barrier, inc=1, device_id={"space": partner}, device_id_type=MESH)

    @pl.when(inner)
    def _():
        opposite = {"tm": 2 * middle - 1 - time, "space": partner_low}
        pl.semaphore_signal(barrier, inc=1, device_id=opposite, device_id_type=MESH)

    for d in (0, 1):
        @pl.when(hopping[d])
        def _():
            ahead = {"tm": inward, "space": space - 1 + 2 * d}
            pl.semaphore_signal(barrier, inc=1, device_id=ahead, device_id_type=MESH)

        @pl.when(hosting[d])
        def _():
            behind = {"tm": guest, "space": space - 1 + 2 * d}
            pl.semaphore_signal(barrier, inc=1, device_id=behind, device_id_type=MESH)

    greeted = len(partners) + sum(has.astype(jnp.int32) for has in has_time + has_space)
    greeted = greeted + inner.astype(jnp.int32)
    greeted = greeted + sum(hop.astype(jnp.int32) for hop in hopping + hosting)

    mine = words.at[core, column, low]
    lanes = [pl.ds(head * HEAD, HEAD) for head in range(HEADS)]
    for head, at in enumerate(lanes):
        pltpu.make_async_copy(text.at[:, :, at], mine.at[head], load_sem.at[2]).start()
    for head, at in enumerate(lanes):
        pltpu.make_async_copy(stale.at[:, :, at], stale_all.at[head], load_sem.at[0]).start()
    for head, at in enumerate(lanes):
        pltpu.make_async_copy(query.at[:, at], q_all.at[head], load_sem.at[1]).start()
    loads = [
        pltpu.make_async_copy(target, target, load_sem.at[i])
        for i, target in enumerate((stale_all, q_all, mine, k_all, v_all))
    ]

    slots = slots_of(window)
    for head in range(HEADS):
        place[head] = jnp.minimum(slots[head], HEADS - 1)
    for s in range(HEADS):
        chosen = jnp.int32(0)
        for head in range(HEADS):
            apart = jnp.maximum(slots[head] - s, s - slots[head])
            chosen = chosen + head * jnp.maximum(1 - apart, 0)
        order[s] = chosen

    def pack(target, base):
        for g in range(GROUP):
            target[:, g] = stale_all[order[base + g]]

    def along_time(kind, d, source, target):
        return pltpu.make_async_remote_copy(
            src_ref=source, dst_ref=target.at[1 - d],
            send_sem=send_sem.at[kind, d], recv_sem=recv_sem.at[kind, 1 - d],
            device_id={"tm": time - 1 + 2 * d}, device_id_type=MESH,
        )

    def along_space(kind, d, source, target):
        return pltpu.make_async_remote_copy(
            src_ref=source, dst_ref=target.at[1 - d],
            send_sem=send_sem.at[kind, d], recv_sem=recv_sem.at[kind, 1 - d],
            device_id={"space": space - 1 + 2 * d}, device_id_type=MESH,
        )

    def send_both(has, make, kind, source, target):
        for d in (0, 1):
            @pl.when(has[d])
            def _():
                make(kind, d, source, target).start()

    def arrived(has, make, kind, source, target):
        for d in (0, 1):
            @pl.when(has[d])
            def _():
                make(kind, 1 - d, source, target).wait_recv()

    def sent(has, make, kind, source, target):
        for d in (0, 1):
            @pl.when(has[d])
            def _():
                make(kind, d, source, target).wait_send()

    spread = [
        pltpu.make_async_remote_copy(
            src_ref=words.at[core, column], dst_ref=words.at[core, column],
            send_sem=text_send.at[d], recv_sem=text_recv.at[d],
            device_id={"space": lax.rem(space + 4 * d, spaces)}, device_id_type=MESH,
        )
        for d in (1, 2, 3)
    ]
    swap = pltpu.make_async_remote_copy(
        src_ref=mine, dst_ref=mine, send_sem=text_send.at[0], recv_sem=text_recv.at[0],
        device_id={"space": partner_low}, device_id_type=MESH,
    )
    loads[2].wait()
    pl.semaphore_wait(barrier, greeted)
    swap.start()
    loads[0].wait()
    pack(pack11, 0)
    send_both(has_time, along_time, 0, pack11, got11)
    for head, at in enumerate(lanes):
        pltpu.make_async_copy(fresh_key.at[:, at], k_all.at[head], load_sem.at[3]).start()
        pltpu.make_async_copy(fresh_value.at[:, at], v_all.at[head], load_sem.at[4]).start()
    swap.wait_recv()
    for copy in spread:
        copy.start()
    loads[1].wait()
    for g in range(GROUP):
        packq[g] = q_all[order[g]]
    send_both(has_space, along_space, 3, packq, gotq)
    pack(pack10, GROUP)

    pieces = [(kv, g) for g in range(GROUP) for kv in range(2)]

    def detour(d, i):
        kv, g = pieces[i]
        return pltpu.make_async_remote_copy(
            src_ref=pack10.at[kv, g], dst_ref=relay.at[kv, g],
            send_sem=send_sem.at[1, d], recv_sem=relay_recv.at[i],
            device_id={"space": partner_low}, device_id_type=MESH,
        )

    def onward(d, i):
        kv, g = pieces[i]
        return pltpu.make_async_remote_copy(
            src_ref=relay.at[kv, g], dst_ref=got10.at[1 - d, kv, g],
            send_sem=relay_send, recv_sem=recv_sem.at[1, 1 - d],
            device_id={"tm": time - 1 + 2 * d, "space": partner_low}, device_id_type=MESH,
        )

    for d in (0, 1):
        @pl.when(bent[d])
        def _():
            for i in range(len(pieces)):
                detour(d, i).start()

    pack(pack01, 2 * GROUP)
    send_both(direct, along_space, 2, pack01, got01)

    def hop(d, i):
        kv, g = pieces[i]
        return pltpu.make_async_remote_copy(
            src_ref=pack01.at[kv, g], dst_ref=hosted.at[kv, g],
            send_sem=send_sem.at[2, d], recv_sem=hosted_recv.at[i],
            device_id={"tm": inward, "space": space - 1 + 2 * d}, device_id_type=MESH,
        )

    def home(d, i):
        kv, g = pieces[i]
        return pltpu.make_async_remote_copy(
            src_ref=hosted.at[kv, g], dst_ref=got01.at[d, kv, g],
            send_sem=hosted_send, recv_sem=recv_sem.at[2, d],
            device_id={"tm": guest}, device_id_type=MESH,
        )

    for d in (0, 1):
        @pl.when(hopping[d])
        def _():
            for i in range(len(pieces)):
                hop(d, i).start()

    def rows_at(block):
        return pl.ds(block * ROW_BLOCK, ROW_BLOCK)

    def attend(jobs):
        for job in jobs:
            job["keys"] = jnp.concatenate([chunk[0] for chunk in job["chunks"]], axis=0)
            values = jnp.concatenate([chunk[1] for chunk in job["chunks"]], axis=0)
            ones = jnp.ones((values.shape[0], LANES), jnp.bfloat16)
            job["values"] = jnp.concatenate([values, ones], axis=1)
        tasks = [dict(job, here=rows_at(block)) for job in jobs for block in range(rows // ROW_BLOCK)]

        def score(task):
            query_rows = task["query"](task["here"])
            task["scores"] = lax.dot_general(
                query_rows, task["keys"], (((1,), (1,)), ((), ())),
                preferred_element_type=jnp.float32,
            ) * scale

        def weigh(task):
            pieces, tops, at = [], [], 0
            before = task["before"](task["here"]) if task["before"] else None
            for keys, _, live, valid in task["chunks"]:
                piece = task["scores"][:, at : at + keys.shape[0]]
                at += keys.shape[0]
                if live is not None:
                    piece = jnp.where(live, piece, -1e30)
                top = jnp.broadcast_to(jnp.max(piece, axis=1, keepdims=True), (ROW_BLOCK, LANES))
                if valid is not None:
                    top = jnp.where(valid, top, -1e30)
                pieces.append(piece)
                tops.append(top)
            top = functools.reduce(jnp.maximum, tops + ([before[0]] if before else []))
            weights = []
            for piece, (_, _, _, valid) in zip(pieces, task["chunks"]):
                base = top if valid is None else jnp.where(valid, top, 1e30)
                base = jnp.concatenate([base] * (piece.shape[1] // LANES), axis=1)
                weights.append(jnp.exp2(piece - base).astype(jnp.bfloat16))
            both = jnp.dot(
                jnp.concatenate(weights, axis=1), task["values"], preferred_element_type=jnp.float32
            )
            mixed, total = both[:, :HEAD], both[:, HEAD:]
            if before:
                shrink = jnp.exp2(before[0] - top)
                total = before[1] * shrink + total
                mixed = before[2] * shrink + mixed
            task["after"](task["here"], top, total, mixed)

        score(tasks[0])
        for i, task in enumerate(tasks):
            if i + 1 < len(tasks):
                score(tasks[i + 1])
            weigh(task)

    def job(query, chunks, after, before=None):
        return {"query": query, "chunks": chunks, "before": before, "after": after}

    def own(slot):
        head = order[slot]
        return lambda here: q_all[head, here]

    def saved(g, state):
        return lambda here: (peak[g][state, here], total[g][state, here], mixed[g][state, here])

    def save(g, state):
        def after(here, top, weight, value):
            peak[g][state, here] = top
            total[g][state, here] = weight
            mixed[g][state, here] = value

        return after

    def finish(target, at):
        def after(here, top, weight, value):
            target[(*at, here)] = (value / weight).astype(jnp.bfloat16)

        return after

    def both_of(first, second):
        def after(*result):
            first(*result)
            second(*result)

        return after

    def fresh(slot):
        head = order[slot]
        return k_all[head], v_all[head], None, None

    def spoken(slot):
        head = order[slot]
        keys = words[:, :, :, head, 0].reshape(count, HEAD)
        values = words[:, :, :, head, 1].reshape(count, HEAD)
        return keys, values, live, None

    def side_ok(d, position, count):
        return jnp.where(d == 0, position > 0, position < count - 1)

    soon_time = jnp.logical_or(time == middle, time == 0).astype(jnp.int32)
    outer = jnp.logical_or(time == 0, time == times - 1)
    soon_space = 1 - core
    ok_time = functools.partial(side_ok, position=time, count=times)
    ok_space = functools.partial(side_ok, position=space, count=spaces)

    def arrived_one(ok, make, kind, d, source, target):
        @pl.when(ok(d))
        def _():
            make(kind, 1 - d, source, target).wait_recv()

    def beside(got, g, d, ok):
        return got[d, 0, g], got[d, 1, g], None, ok(d)

    count = 2 * spaces // 2 * words.shape[5]
    index = lax.broadcasted_iota(jnp.int32, (1, count), 1)
    token = (((index // 32) % 4) * 4 + ((index // 16) % 2) * 2 + index // 128) * 16 + index % 16
    live = token < text_len[0]

    for d in (0, 1):
        @pl.when(jnp.logical_not(has_time[d]))
        def _():
            got11[d] = jnp.zeros_like(got11[d])
            got10[d] = jnp.zeros_like(got10[d])

        @pl.when(jnp.logical_not(has_space[d]))
        def _():
            got01[d] = jnp.zeros_like(got01[d])
            o_got[d] = jnp.zeros_like(o_got[d])
            o_got_stat[d] = jnp.full_like(o_got_stat[d], -1e30)

    loads[3].wait()
    loads[4].wait()

    @pl.loop(0, 3)
    def _(kind):
        attend([
            job(own(kind * GROUP + g), [fresh(kind * GROUP + g)], save(g, kind))
            for g in range(GROUP)
        ])

    arrived(has_space, along_space, 3, packq, gotq)

    def visitor(d, g):
        return lambda here: gotq[d, g, here]

    @pl.loop(0, 2)
    def _(d):
        @pl.when(side_ok(d, space, spaces))
        def _():
            attend([
                job(visitor(d, g), [(pack11[0, g], pack11[1, g], None, None)], save(g, 3 + d))
                for g in range(GROUP)
            ])

    for d in (0, 1):
        @pl.when(straight[d])
        def _():
            along_time(0, d, pack11, got11).wait_send()
            along_time(1, d, pack10, got10).start()

    for d in (0, 1):
        @pl.when(bent[d])
        def _():
            for i in range(len(pieces)):
                detour(d, i).wait_recv()
                onward(d, i).start()

    for copy in spread:
        copy.wait_recv()
    half = words.at[core]
    across = pltpu.make_async_remote_copy(
        src_ref=half, dst_ref=half, send_sem=text_send.at[4], recv_sem=text_recv.at[4],
        device_id={"space": sibling}, device_id_type=MESH,
    )
    across.start()

    arrived_one(ok_time, along_time, 0, soon_time, pack11, got11)
    lane = lax.broadcasted_iota(jnp.int32, (rows, LANES), 1)

    arrived_one(ok_time, along_time, 0, 1 - soon_time, pack11, got11)

    def answer(frames):
        @pl.loop(0, 2)
        def _(i):
            d = lax.rem(i + core, 2)

            @pl.when(side_ok(d, space, spaces))
            def _():
                def give(g):
                    def after(here, top, weight, value):
                        o_send[d, g, here] = (value / weight).astype(jnp.bfloat16)
                        peak[g][3 + d, here] = top + jnp.log2(weight)

                    return after

                attend([
                    job(visitor(d, g), [beside(got11, g, e, ok_time) for e in frames], give(g), saved(g, 3 + d))
                    for g in range(GROUP)
                ])
                stats = jnp.zeros((rows, LANES), jnp.float32)
                for g in range(GROUP):
                    stats = jnp.where(lane == g, peak[g][3 + d], stats)
                o_stat[d] = stats.T[:8]
                along_space(4, d, o_send.at[d], o_got).start()
                along_space(5, d, o_stat.at[d], o_got_stat).start()

    pl.when(outer)(lambda: answer((soon_time,)))
    pl.when(jnp.logical_not(outer))(lambda: answer((0, 1)))

    for d in (0, 1):
        @pl.when(hosting[d])
        def _():
            for i in range(len(pieces)):
                hop(d, i).wait_recv()
                home(d, i).start()

    across.wait_recv()
    attend([
        job(own(3 * GROUP + g), [fresh(3 * GROUP + g), spoken(3 * GROUP + g)], finish(done, (3 * GROUP + g,)))
        for g in range(GROUP)
    ])

    def own_both(frames):
        attend([
            job(own(g), [spoken(g)] + [beside(got11, g, e, ok_time) for e in frames], save(g, 0), saved(g, 0))
            for g in range(GROUP)
        ])

    pl.when(outer)(lambda: own_both((soon_time,)))
    pl.when(jnp.logical_not(outer))(lambda: own_both((0, 1)))
    def side(k, soon):
        first = jnp.where(k == 0, soon_time, soon_space)
        return first if soon else 1 - first

    def arrived_side(k, d):
        @pl.when(k == 0)
        def _():
            arrived_one(ok_time, along_time, 1, d, pack10, got10)

        @pl.when(k == 1)
        def _():
            arrived_one(ok_space, along_space, 2, d, pack01, got01)

    def beside_of(k, g, d):
        ok = jnp.where(k == 0, ok_time(d), ok_space(d))
        return got_sides[k, d, 0, g], got_sides[k, d, 1, g], None, ok

    @pl.loop(0, 2)
    def _(i):
        k = 1 - i
        d = side(k, True)
        arrived_side(k, d)
        attend([
            job(
                own((1 + k) * GROUP + g), [spoken((1 + k) * GROUP + g), beside_of(k, g, d)],
                both_of(save(g, 1 + k), finish(done, ((1 + k) * GROUP + g,))), saved(g, 1 + k),
            )
            for g in range(GROUP)
        ])

    @pl.loop(0, 2)
    def _(i):
        k = jnp.where(outer, i, 1 - i)
        d = side(k, False)
        arrived_side(k, d)

        @pl.when(jnp.where(k == 0, ok_time(d), ok_space(d)))
        def _():
            attend([
                job(
                    own((1 + k) * GROUP + g), [beside_of(k, g, d)],
                    finish(done, ((1 + k) * GROUP + g,)), saved(g, 1 + k),
                )
                for g in range(GROUP)
            ])

    logs = []
    for d in (0, 1):
        @pl.when(has_space[d])
        def _():
            along_space(4, 1 - d, o_send.at[1 - d], o_got).wait_recv()
            along_space(5, 1 - d, o_stat.at[1 - d], o_got_stat).wait_recv()

        spare = jnp.zeros((LANES - 8, rows), jnp.float32)
        logs.append(jnp.concatenate([o_got_stat[d], spare], axis=0).T)
    for g in range(GROUP):
        others = [jnp.broadcast_to(log[:, g : g + 1], (rows, LANES)) for log in logs]
        top = jnp.maximum(peak[g][0], jnp.maximum(*others))
        keep = jnp.exp2(peak[g][0] - top)
        add = [jnp.exp2(other - top) for other in others]
        value = mixed[g][0] * keep
        for d in (0, 1):
            value = value + o_got[d, g].astype(jnp.float32) * add[d]
        done[g] = (value / (total[g][0] * keep + add[0] + add[1])).astype(jnp.bfloat16)

    for head in range(HEADS):
        out_all[:, head * HEAD : (head + 1) * HEAD] = done[place[head]]
    store = pltpu.make_async_copy(out_all, out, load_sem.at[5])
    store.start()

    for d in (0, 1):
        @pl.when(bent[d])
        def _():
            along_time(0, d, pack11, got11).wait_send()

    sent(has_time, along_time, 1, pack10, got10)

    @pl.when(inner)
    def _():
        pltpu.make_async_copy(relay, relay, relay_send).wait()

    @pl.when(jnp.logical_or(*hosting))
    def _():
        pltpu.make_async_copy(hosted, hosted, hosted_send).wait()

    sent(has_space, along_space, 2, pack01, got01)
    sent(has_space, along_space, 3, packq, gotq)
    for d in (0, 1):
        @pl.when(has_space[d])
        def _():
            along_space(4, d, o_send.at[d], o_got).wait_send()
            along_space(5, d, o_stat.at[d], o_got_stat).wait_send()
    swap.wait_send()
    for copy in spread:
        copy.wait_send()
    across.wait_send()
    store.wait()


def on_device(query, fresh_key, fresh_value, stale_kv, text_kv, window, text_len):
    rows, width = query.shape[2:]
    words = text_kv.shape[1]
    bf16, f32 = jnp.bfloat16, jnp.float32
    heads = (GROUP, rows, HEAD)
    scalars = pl.BlockSpec(memory_space=pltpu.SMEM)
    result = pl.pallas_call(
        kernel,
        out_shape=jax.ShapeDtypeStruct((rows, width), bf16),
        in_specs=[pl.BlockSpec(memory_space=pltpu.HBM)] * 5 + [scalars] * 2,
        out_specs=pl.BlockSpec(memory_space=pl.ANY),
        scratch_shapes=[
            pltpu.VMEM((HEADS, rows, HEAD), bf16),
            pltpu.VMEM((HEADS, rows, HEAD), bf16),
            pltpu.VMEM((HEADS, rows, HEAD), bf16),
            pltpu.VMEM((HEADS, 2, rows, HEAD), bf16),
            pltpu.VMEM((2, 4, 2, HEADS, 2, words, HEAD), bf16),
            pltpu.VMEM((rows, width), bf16),
            pltpu.VMEM((2, *heads), bf16),
            pltpu.VMEM((2, 2, *heads), bf16),
            pltpu.VMEM(heads, bf16),
            pltpu.VMEM((2, 2, *heads), bf16),
            pltpu.VMEM((2, 2, 2, *heads), bf16),
            pltpu.VMEM((2, *heads), bf16),
            pltpu.VMEM((2, *heads), bf16),
            pltpu.VMEM((2, 8, rows), f32),
            pltpu.VMEM((2, *heads), bf16),
            pltpu.VMEM((2, 8, rows), f32),
            [pltpu.VMEM((5, rows, LANES), f32)] * GROUP,
            [pltpu.VMEM((5, rows, LANES), f32)] * GROUP,
            [pltpu.VMEM((5, rows, HEAD), f32)] * GROUP,
            pltpu.VMEM((HEADS, rows, HEAD), bf16),
            pltpu.SMEM((HEADS,), jnp.int32),
            pltpu.SMEM((HEADS,), jnp.int32),
            pltpu.VMEM((2, *heads), bf16),
            pltpu.VMEM((2, *heads), bf16),
            pltpu.SemaphoreType.DMA((6,)),
            pltpu.SemaphoreType.DMA((6, 2)),
            pltpu.SemaphoreType.DMA((6, 2)),
            pltpu.SemaphoreType.DMA((5,)),
            pltpu.SemaphoreType.DMA((5,)),
            pltpu.SemaphoreType.DMA(()),
            pltpu.SemaphoreType.DMA((2 * GROUP,)),
            pltpu.SemaphoreType.DMA(()),
            pltpu.SemaphoreType.DMA((2 * GROUP,)),
        ],
        compiler_params=pltpu.CompilerParams(
            collective_id=0, has_side_effects=True, vmem_limit_bytes=52 << 20
        ),
    )(
        query[0, 0], fresh_key[0, 0], fresh_value[0, 0], stale_kv[:, 0, 0], text_kv,
        window.T, text_len,
    )
    return result[None, None]


def solution(mesh):
    in_specs = (
        P("tm", "space", None, None),
        P("tm", "space", None, None),
        P("tm", "space", None, None),
        P(None, "tm", "space", None, None),
        P(None, "space", None),
        P(),
        P(),
    )
    out_specs = P("tm", "space", None, None)
    return jax.shard_map(
        on_device, mesh=mesh, in_specs=in_specs, out_specs=out_specs, check_vma=False
    )
```

```python
import functools
import math

import jax
import jax.numpy as jnp
from jax import lax
from jax.experimental import pallas as pl
from jax.experimental.pallas import tpu as pltpu
from jax.sharding import PartitionSpec as P

MESH = pl.DeviceIdType.MESH
HEAD = 128
GROUP = 3
HEADS = 12
LANES = 128
ROW_BLOCK = 384


def slots_of(window):
    counts = [jnp.int32(0)] * 4
    slots = []
    for head in range(HEADS):
        reach_time, reach_space = window[0, head], window[1, head]
        both = reach_time * reach_space
        hits = [both, reach_time - both, reach_space - both, 1 - reach_time - reach_space + both]
        slot = jnp.int32(0)
        for k in range(4):
            slot = slot + hits[k] * (GROUP * k + counts[k])
            counts[k] = counts[k] + hits[k]
        slots.append(slot)
    return slots


def kernel(
    query, fresh_key, fresh_value, stale, text, window, text_len, out,
    q_all, k_all, v_all, stale_all, words, out_all,
    pack11, sides, packq,
    got11, got_sides, gotq,
    o_send, o_stat, o_got, o_got_stat,
    peak, total, mixed, done, order, place,
    relay, hosted, load_sem, send_sem, recv_sem, text_send, text_recv, relay_send, relay_recv, hosted_send, hosted_recv,
):
    rows = q_all.shape[1]
    pack10, pack01 = sides.at[0], sides.at[1]
    got10, got01 = got_sides.at[0], got_sides.at[1]
    times = lax.axis_size("tm")
    spaces = lax.axis_size("space")
    time = lax.axis_index("tm")
    space = lax.axis_index("space")
    core = lax.rem(space, 2)
    low = lax.rem(space // 2, 2)
    column = space // 4
    has_time = (time > 0, time < times - 1)
    has_space = (space > 0, space < spaces - 1)
    next_time = (time - 1, time + 1)
    next_space = (space - 1, space + 1)
    middle = times // 2
    inner = jnp.logical_or(time == middle - 1, time == middle)
    straight = (
        jnp.logical_and(has_time[0], time != middle),
        jnp.logical_and(has_time[1], time != middle - 1),
    )
    bent = (time == middle, time == middle - 1)
    loaded = jnp.logical_or(jnp.logical_or(time == 0, time == times - 1), inner)
    inward = jnp.where(jnp.logical_or(time == 0, time == middle), time + 1, time - 1)
    host = functools.reduce(
        jnp.logical_or, [time == 1, time == middle - 2, time == middle + 1, time == times - 2]
    )
    guest = jnp.where(jnp.logical_or(time == 1, time == middle + 1), time - 1, time + 1)
    crossing = (
        jnp.logical_and(has_space[0], lax.rem(space, 4) == 0),
        jnp.logical_and(has_space[1], lax.rem(space, 4) == 3),
    )
    hopping = [jnp.logical_and(loaded, crossing[d]) for d in (0, 1)]
    hosting = [jnp.logical_and(host, crossing[d]) for d in (0, 1)]
    direct = [jnp.logical_and(has_space[d], jnp.logical_not(hopping[d])) for d in (0, 1)]
    scale = math.log2(math.e) / math.sqrt(HEAD)

    partner_low = column * 4 + (1 - low) * 2 + core
    sibling = space + 1 - 2 * core
    barrier = pltpu.get_barrier_semaphore()
    for d in (0, 1):
        @pl.when(has_time[d])
        def _():
            pl.semaphore_signal(barrier, inc=1, device_id={"tm": time - 1 + 2 * d}, device_id_type=MESH)

        @pl.when(has_space[d])
        def _():
            pl.semaphore_signal(barrier, inc=1, device_id={"space": space - 1 + 2 * d}, device_id_type=MESH)

    partners = [partner_low] + [lax.rem(space + 4 * d, spaces) for d in (1, 2, 3)]
    for partner in partners:
        pl.semaphore_signal(barrier, inc=1, device_id={"space": partner}, device_id_type=MESH)

    @pl.when(inner)
    def _():
        opposite = {"tm": 2 * middle - 1 - time, "space": partner_low}
        pl.semaphore_signal(barrier, inc=1, device_id=opposite, device_id_type=MESH)

    for d in (0, 1):
        @pl.when(hopping[d])
        def _():
            ahead = {"tm": inward, "space": space - 1 + 2 * d}
            pl.semaphore_signal(barrier, inc=1, device_id=ahead, device_id_type=MESH)

        @pl.when(hosting[d])
        def _():
            behind = {"tm": guest, "space": space - 1 + 2 * d}
            pl.semaphore_signal(barrier, inc=1, device_id=behind, device_id_type=MESH)

    greeted = len(partners) + sum(has.astype(jnp.int32) for has in has_time + has_space)
    greeted = greeted + inner.astype(jnp.int32)
    greeted = greeted + sum(hop.astype(jnp.int32) for hop in hopping + hosting)

    mine = words.at[core, column, low]
    lanes = [pl.ds(head * HEAD, HEAD) for head in range(HEADS)]
    for head, at in enumerate(lanes):
        pltpu.make_async_copy(text.at[:, :, at], mine.at[head], load_sem.at[2]).start()
    for head, at in enumerate(lanes):
        pltpu.make_async_copy(stale.at[:, :, at], stale_all.at[head], load_sem.at[0]).start()
    for head, at in enumerate(lanes):
        pltpu.make_async_copy(query.at[:, at], q_all.at[head], load_sem.at[1]).start()
    loads = [
        pltpu.make_async_copy(target, target, load_sem.at[i])
        for i, target in enumerate((stale_all, q_all, mine, k_all, v_all))
    ]

    slots = slots_of(window)
    for head in range(HEADS):
        place[head] = jnp.minimum(slots[head], HEADS - 1)
    for s in range(HEADS):
        chosen = jnp.int32(0)
        for head in range(HEADS):
            apart = jnp.maximum(slots[head] - s, s - slots[head])
            chosen = chosen + head * jnp.maximum(1 - apart, 0)
        order[s] = chosen

    def pack(target, base):
        for g in range(GROUP):
            target[:, g] = stale_all[order[base + g]]

    def along_time(kind, d, source, target):
        return pltpu.make_async_remote_copy(
            src_ref=source, dst_ref=target.at[1 - d],
            send_sem=send_sem.at[kind, d], recv_sem=recv_sem.at[kind, 1 - d],
            device_id={"tm": time - 1 + 2 * d}, device_id_type=MESH,
        )

    def along_space(kind, d, source, target):
        return pltpu.make_async_remote_copy(
            src_ref=source, dst_ref=target.at[1 - d],
            send_sem=send_sem.at[kind, d], recv_sem=recv_sem.at[kind, 1 - d],
            device_id={"space": space - 1 + 2 * d}, device_id_type=MESH,
        )

    def send_both(has, make, kind, source, target):
        for d in (0, 1):
            @pl.when(has[d])
            def _():
                make(kind, d, source, target).start()

    def arrived(has, make, kind, source, target):
        for d in (0, 1):
            @pl.when(has[d])
            def _():
                make(kind, 1 - d, source, target).wait_recv()

    def sent(has, make, kind, source, target):
        for d in (0, 1):
            @pl.when(has[d])
            def _():
                make(kind, d, source, target).wait_send()

    spread = [
        pltpu.make_async_remote_copy(
            src_ref=words.at[core, column], dst_ref=words.at[core, column],
            send_sem=text_send.at[d], recv_sem=text_recv.at[d],
            device_id={"space": lax.rem(space + 4 * d, spaces)}, device_id_type=MESH,
        )
        for d in (1, 2, 3)
    ]
    swap = pltpu.make_async_remote_copy(
        src_ref=mine, dst_ref=mine, send_sem=text_send.at[0], recv_sem=text_recv.at[0],
        device_id={"space": partner_low}, device_id_type=MESH,
    )
    loads[2].wait()
    pl.semaphore_wait(barrier, greeted)
    swap.start()
    def spread_text():
        swap.wait_recv()
        for copy in spread:
            copy.start()

    pl.when(loaded)(spread_text)
    loads[0].wait()
    pack(pack11, 0)
    send_both(has_time, along_time, 0, pack11, got11)
    for head, at in enumerate(lanes):
        pltpu.make_async_copy(fresh_key.at[:, at], k_all.at[head], load_sem.at[3]).start()
        pltpu.make_async_copy(fresh_value.at[:, at], v_all.at[head], load_sem.at[4]).start()
    pl.when(jnp.logical_not(loaded))(spread_text)
    loads[1].wait()
    for g in range(GROUP):
        packq[g] = q_all[order[g]]
    send_both(has_space, along_space, 3, packq, gotq)
    pack(pack10, GROUP)

    pieces = [(kv, g) for g in range(GROUP) for kv in range(2)]

    def detour(d, i):
        kv, g = pieces[i]
        return pltpu.make_async_remote_copy(
            src_ref=pack10.at[kv, g], dst_ref=relay.at[kv, g],
            send_sem=send_sem.at[1, d], recv_sem=relay_recv.at[i],
            device_id={"space": partner_low}, device_id_type=MESH,
        )

    def onward(d, i):
        kv, g = pieces[i]
        return pltpu.make_async_remote_copy(
            src_ref=relay.at[kv, g], dst_ref=got10.at[1 - d, kv, g],
            send_sem=relay_send, recv_sem=recv_sem.at[1, 1 - d],
            device_id={"tm": time - 1 + 2 * d, "space": partner_low}, device_id_type=MESH,
        )

    for d in (0, 1):
        @pl.when(bent[d])
        def _():
            for i in range(len(pieces)):
                detour(d, i).start()

    pack(pack01, 2 * GROUP)
    send_both(direct, along_space, 2, pack01, got01)

    def hop(d, i):
        kv, g = pieces[i]
        return pltpu.make_async_remote_copy(
            src_ref=pack01.at[kv, g], dst_ref=hosted.at[kv, g],
            send_sem=send_sem.at[2, d], recv_sem=hosted_recv.at[i],
            device_id={"tm": inward, "space": space - 1 + 2 * d}, device_id_type=MESH,
        )

    def home(d, i):
        kv, g = pieces[i]
        return pltpu.make_async_remote_copy(
            src_ref=hosted.at[kv, g], dst_ref=got01.at[d, kv, g],
            send_sem=hosted_send, recv_sem=recv_sem.at[2, d],
            device_id={"tm": guest}, device_id_type=MESH,
        )

    for d in (0, 1):
        @pl.when(hopping[d])
        def _():
            for i in range(len(pieces)):
                hop(d, i).start()

    def rows_at(block):
        return pl.ds(block * ROW_BLOCK, ROW_BLOCK)

    def attend(jobs):
        for job in jobs:
            job["keys"] = jnp.concatenate([chunk[0] for chunk in job["chunks"]], axis=0)
            values = jnp.concatenate([chunk[1] for chunk in job["chunks"]], axis=0)
            ones = jnp.ones((values.shape[0], LANES), jnp.bfloat16)
            job["values"] = jnp.concatenate([values, ones], axis=1)
        tasks = [dict(job, here=rows_at(block)) for job in jobs for block in range(rows // ROW_BLOCK)]

        def score(task):
            query_rows = task["query"](task["here"])
            task["scores"] = lax.dot_general(
                query_rows, task["keys"], (((1,), (1,)), ((), ())),
                preferred_element_type=jnp.float32,
            ) * scale

        def weigh(task):
            pieces, tops, at = [], [], 0
            before = task["before"](task["here"]) if task["before"] else None
            for keys, _, live, valid in task["chunks"]:
                piece = task["scores"][:, at : at + keys.shape[0]]
                at += keys.shape[0]
                if live is not None:
                    piece = jnp.where(live, piece, -1e30)
                top = jnp.broadcast_to(jnp.max(piece, axis=1, keepdims=True), (ROW_BLOCK, LANES))
                if valid is not None:
                    top = jnp.where(valid, top, -1e30)
                pieces.append(piece)
                tops.append(top)
            top = functools.reduce(jnp.maximum, tops + ([before[0]] if before else []))
            weights = []
            for piece, (_, _, _, valid) in zip(pieces, task["chunks"]):
                base = top if valid is None else jnp.where(valid, top, 1e30)
                base = jnp.concatenate([base] * (piece.shape[1] // LANES), axis=1)
                weights.append(jnp.exp2(piece - base).astype(jnp.bfloat16))
            both = jnp.dot(
                jnp.concatenate(weights, axis=1), task["values"], preferred_element_type=jnp.float32
            )
            mixed, total = both[:, :HEAD], both[:, HEAD:]
            if before:
                shrink = jnp.exp2(before[0] - top)
                total = before[1] * shrink + total
                mixed = before[2] * shrink + mixed
            task["after"](task["here"], top, total, mixed)

        score(tasks[0])
        for i, task in enumerate(tasks):
            if i + 1 < len(tasks):
                score(tasks[i + 1])
            weigh(task)

    def job(query, chunks, after, before=None):
        return {"query": query, "chunks": chunks, "before": before, "after": after}

    def own(slot):
        head = order[slot]
        return lambda here: q_all[head, here]

    def saved(g, state):
        return lambda here: (peak[g][state, here], total[g][state, here], mixed[g][state, here])

    def save(g, state):
        def after(here, top, weight, value):
            peak[g][state, here] = top
            total[g][state, here] = weight
            mixed[g][state, here] = value

        return after

    def finish(target, at):
        def after(here, top, weight, value):
            target[(*at, here)] = (value / weight).astype(jnp.bfloat16)

        return after

    def both_of(first, second):
        def after(*result):
            first(*result)
            second(*result)

        return after

    def fresh(slot):
        head = order[slot]
        return k_all[head], v_all[head], None, None

    def spoken(slot):
        head = order[slot]
        keys = words[:, :, :, head, 0].reshape(count, HEAD)
        values = words[:, :, :, head, 1].reshape(count, HEAD)
        return keys, values, live, None

    def side_ok(d, position, count):
        return jnp.where(d == 0, position > 0, position < count - 1)

    soon_time = jnp.logical_or(time == middle, time == 0).astype(jnp.int32)
    outer = jnp.logical_or(time == 0, time == times - 1)
    soon_space = 1 - core
    ok_time = functools.partial(side_ok, position=time, count=times)
    ok_space = functools.partial(side_ok, position=space, count=spaces)

    def arrived_one(ok, make, kind, d, source, target):
        @pl.when(ok(d))
        def _():
            make(kind, 1 - d, source, target).wait_recv()

    def beside(got, g, d, ok):
        return got[d, 0, g], got[d, 1, g], None, ok(d)

    count = 2 * spaces // 2 * words.shape[5]
    index = lax.broadcasted_iota(jnp.int32, (1, count), 1)
    token = (((index // 32) % 4) * 4 + ((index // 16) % 2) * 2 + index // 128) * 16 + index % 16
    live = token < text_len[0]

    for d in (0, 1):
        @pl.when(jnp.logical_not(has_time[d]))
        def _():
            got11[d] = jnp.zeros_like(got11[d])
            got10[d] = jnp.zeros_like(got10[d])

        @pl.when(jnp.logical_not(has_space[d]))
        def _():
            got01[d] = jnp.zeros_like(got01[d])
            o_got[d] = jnp.zeros_like(o_got[d])
            o_got_stat[d] = jnp.full_like(o_got_stat[d], -1e30)

    loads[3].wait()
    loads[4].wait()

    @pl.loop(0, 3)
    def _(kind):
        attend([
            job(own(kind * GROUP + g), [fresh(kind * GROUP + g)], save(g, kind))
            for g in range(GROUP)
        ])

    arrived(has_space, along_space, 3, packq, gotq)

    def visitor(d, g):
        return lambda here: gotq[d, g, here]

    @pl.loop(0, 2)
    def _(d):
        @pl.when(side_ok(d, space, spaces))
        def _():
            attend([
                job(visitor(d, g), [(pack11[0, g], pack11[1, g], None, None)], save(g, 3 + d))
                for g in range(GROUP)
            ])

    for d in (0, 1):
        @pl.when(straight[d])
        def _():
            along_time(0, d, pack11, got11).wait_send()
            along_time(1, d, pack10, got10).start()

    for d in (0, 1):
        @pl.when(bent[d])
        def _():
            for i in range(len(pieces)):
                detour(d, i).wait_recv()
                onward(d, i).start()

    for copy in spread:
        copy.wait_recv()
    half = words.at[core]
    across = pltpu.make_async_remote_copy(
        src_ref=half, dst_ref=half, send_sem=text_send.at[4], recv_sem=text_recv.at[4],
        device_id={"space": sibling}, device_id_type=MESH,
    )
    across.start()

    arrived_one(ok_time, along_time, 0, soon_time, pack11, got11)
    lane = lax.broadcasted_iota(jnp.int32, (rows, LANES), 1)

    arrived_one(ok_time, along_time, 0, 1 - soon_time, pack11, got11)

    def answer(frames):
        @pl.loop(0, 2)
        def _(i):
            d = lax.rem(i + core, 2)

            @pl.when(side_ok(d, space, spaces))
            def _():
                def give(g):
                    def after(here, top, weight, value):
                        o_send[d, g, here] = (value / weight).astype(jnp.bfloat16)
                        peak[g][3 + d, here] = top + jnp.log2(weight)

                    return after

                attend([
                    job(visitor(d, g), [beside(got11, g, e, ok_time) for e in frames], give(g), saved(g, 3 + d))
                    for g in range(GROUP)
                ])
                stats = jnp.zeros((rows, LANES), jnp.float32)
                for g in range(GROUP):
                    stats = jnp.where(lane == g, peak[g][3 + d], stats)
                o_stat[d] = stats.T[:8]
                along_space(4, d, o_send.at[d], o_got).start()
                along_space(5, d, o_stat.at[d], o_got_stat).start()

    pl.when(outer)(lambda: answer((soon_time,)))
    pl.when(jnp.logical_not(outer))(lambda: answer((0, 1)))

    for d in (0, 1):
        @pl.when(hosting[d])
        def _():
            for i in range(len(pieces)):
                hop(d, i).wait_recv()
                home(d, i).start()

    across.wait_recv()
    attend([
        job(own(3 * GROUP + g), [fresh(3 * GROUP + g), spoken(3 * GROUP + g)], finish(done, (3 * GROUP + g,)))
        for g in range(GROUP)
    ])

    def own_both(frames):
        attend([
            job(own(g), [spoken(g)] + [beside(got11, g, e, ok_time) for e in frames], save(g, 0), saved(g, 0))
            for g in range(GROUP)
        ])

    pl.when(outer)(lambda: own_both((soon_time,)))
    pl.when(jnp.logical_not(outer))(lambda: own_both((0, 1)))
    def side(k, soon):
        first = jnp.where(k == 0, soon_time, soon_space)
        return first if soon else 1 - first

    def arrived_side(k, d):
        @pl.when(k == 0)
        def _():
            arrived_one(ok_time, along_time, 1, d, pack10, got10)

        @pl.when(k == 1)
        def _():
            arrived_one(ok_space, along_space, 2, d, pack01, got01)

    def beside_of(k, g, d):
        ok = jnp.where(k == 0, ok_time(d), ok_space(d))
        return got_sides[k, d, 0, g], got_sides[k, d, 1, g], None, ok

    @pl.loop(0, 2)
    def _(i):
        k = 1 - i
        d = side(k, True)
        arrived_side(k, d)
        attend([
            job(
                own((1 + k) * GROUP + g), [spoken((1 + k) * GROUP + g), beside_of(k, g, d)],
                both_of(save(g, 1 + k), finish(done, ((1 + k) * GROUP + g,))), saved(g, 1 + k),
            )
            for g in range(GROUP)
        ])

    @pl.loop(0, 2)
    def _(i):
        k = jnp.where(outer, i, 1 - i)
        d = side(k, False)
        arrived_side(k, d)

        @pl.when(jnp.where(k == 0, ok_time(d), ok_space(d)))
        def _():
            attend([
                job(
                    own((1 + k) * GROUP + g), [beside_of(k, g, d)],
                    finish(done, ((1 + k) * GROUP + g,)), saved(g, 1 + k),
                )
                for g in range(GROUP)
            ])

    logs = []
    for d in (0, 1):
        @pl.when(has_space[d])
        def _():
            along_space(4, 1 - d, o_send.at[1 - d], o_got).wait_recv()
            along_space(5, 1 - d, o_stat.at[1 - d], o_got_stat).wait_recv()

        spare = jnp.zeros((LANES - 8, rows), jnp.float32)
        logs.append(jnp.concatenate([o_got_stat[d], spare], axis=0).T)
    for g in range(GROUP):
        others = [jnp.broadcast_to(log[:, g : g + 1], (rows, LANES)) for log in logs]
        top = jnp.maximum(peak[g][0], jnp.maximum(*others))
        keep = jnp.exp2(peak[g][0] - top)
        add = [jnp.exp2(other - top) for other in others]
        value = mixed[g][0] * keep
        for d in (0, 1):
            value = value + o_got[d, g].astype(jnp.float32) * add[d]
        done[g] = (value / (total[g][0] * keep + add[0] + add[1])).astype(jnp.bfloat16)

    for head in range(HEADS):
        out_all[:, head * HEAD : (head + 1) * HEAD] = done[place[head]]
    store = pltpu.make_async_copy(out_all, out, load_sem.at[5])
    store.start()

    for d in (0, 1):
        @pl.when(bent[d])
        def _():
            along_time(0, d, pack11, got11).wait_send()

    sent(has_time, along_time, 1, pack10, got10)

    @pl.when(inner)
    def _():
        pltpu.make_async_copy(relay, relay, relay_send).wait()

    @pl.when(jnp.logical_or(*hosting))
    def _():
        pltpu.make_async_copy(hosted, hosted, hosted_send).wait()

    sent(has_space, along_space, 2, pack01, got01)
    sent(has_space, along_space, 3, packq, gotq)
    for d in (0, 1):
        @pl.when(has_space[d])
        def _():
            along_space(4, d, o_send.at[d], o_got).wait_send()
            along_space(5, d, o_stat.at[d], o_got_stat).wait_send()
    swap.wait_send()
    for copy in spread:
        copy.wait_send()
    across.wait_send()
    store.wait()


def on_device(query, fresh_key, fresh_value, stale_kv, text_kv, window, text_len):
    rows, width = query.shape[2:]
    words = text_kv.shape[1]
    bf16, f32 = jnp.bfloat16, jnp.float32
    heads = (GROUP, rows, HEAD)
    scalars = pl.BlockSpec(memory_space=pltpu.SMEM)
    result = pl.pallas_call(
        kernel,
        out_shape=jax.ShapeDtypeStruct((rows, width), bf16),
        in_specs=[pl.BlockSpec(memory_space=pltpu.HBM)] * 5 + [scalars] * 2,
        out_specs=pl.BlockSpec(memory_space=pl.ANY),
        scratch_shapes=[
            pltpu.VMEM((HEADS, rows, HEAD), bf16),
            pltpu.VMEM((HEADS, rows, HEAD), bf16),
            pltpu.VMEM((HEADS, rows, HEAD), bf16),
            pltpu.VMEM((HEADS, 2, rows, HEAD), bf16),
            pltpu.VMEM((2, 4, 2, HEADS, 2, words, HEAD), bf16),
            pltpu.VMEM((rows, width), bf16),
            pltpu.VMEM((2, *heads), bf16),
            pltpu.VMEM((2, 2, *heads), bf16),
            pltpu.VMEM(heads, bf16),
            pltpu.VMEM((2, 2, *heads), bf16),
            pltpu.VMEM((2, 2, 2, *heads), bf16),
            pltpu.VMEM((2, *heads), bf16),
            pltpu.VMEM((2, *heads), bf16),
            pltpu.VMEM((2, 8, rows), f32),
            pltpu.VMEM((2, *heads), bf16),
            pltpu.VMEM((2, 8, rows), f32),
            [pltpu.VMEM((5, rows, LANES), f32)] * GROUP,
            [pltpu.VMEM((5, rows, LANES), f32)] * GROUP,
            [pltpu.VMEM((5, rows, HEAD), f32)] * GROUP,
            pltpu.VMEM((HEADS, rows, HEAD), bf16),
            pltpu.SMEM((HEADS,), jnp.int32),
            pltpu.SMEM((HEADS,), jnp.int32),
            pltpu.VMEM((2, *heads), bf16),
            pltpu.VMEM((2, *heads), bf16),
            pltpu.SemaphoreType.DMA((6,)),
            pltpu.SemaphoreType.DMA((6, 2)),
            pltpu.SemaphoreType.DMA((6, 2)),
            pltpu.SemaphoreType.DMA((5,)),
            pltpu.SemaphoreType.DMA((5,)),
            pltpu.SemaphoreType.DMA(()),
            pltpu.SemaphoreType.DMA((2 * GROUP,)),
            pltpu.SemaphoreType.DMA(()),
            pltpu.SemaphoreType.DMA((2 * GROUP,)),
        ],
        compiler_params=pltpu.CompilerParams(
            collective_id=0, has_side_effects=True, vmem_limit_bytes=52 << 20
        ),
    )(
        query[0, 0], fresh_key[0, 0], fresh_value[0, 0], stale_kv[:, 0, 0], text_kv,
        window.T, text_len,
    )
    return result[None, None]


def solution(mesh):
    in_specs = (
        P("tm", "space", None, None),
        P("tm", "space", None, None),
        P("tm", "space", None, None),
        P(None, "tm", "space", None, None),
        P(None, "space", None),
        P(),
        P(),
    )
    out_specs = P("tm", "space", None, None)
    return jax.shard_map(
        on_device, mesh=mesh, in_specs=in_specs, out_specs=out_specs, check_vma=False
    )
```
